512 devices in a mesh: rep: 16 (over z, y_lo), gy: 8 (over y_hi, core), gz: 4 (over x).
Axes of the slice: x: 4, y: 8 (y_hi: 4, y_lo: 2; y = y_hi * 2 + y_lo), z: 8, core: 2. Of those that a mesh axis runs over, the one named last changes fastest.
Arguments:
- charges: float32 [4096, 256, 128], P(('rep', 'gz'), 'gy'), may hold values from -6 to 6
- green: float32 [256, 256, 128], P('rep', ('gy', 'gz')), may hold values from 0.1 to 3
Outputs:
- potential: float32 [4096, 256, 128], P(('rep', 'gz'), 'gy')
The draws below stay inside these ranges and needn't reach their ends.
All inputs are finite; a program needn't handle non-finite values.
Results may differ from the reference program's by a relative error of at most 0.00007.
Values sent between devices are 32-bit elements; how exact they have to be, the bound alone decides.
No kernel may reach another device: no remote copies, remote signals or barrier semaphores. Data moves between devices by JAX's collectives and lax.ppermute only.
A program may use at most 64 MiB of HBM per device.

```python
import math
import jax
import jax.numpy as jnp
from jax import lax

NG = 256
NZ = 128
REPLICAS = 16


def levels(key, dims, shards, low, top_value):
    gain = 1.0
    for axis_at, blocks in shards:
        steps = jax.random.uniform(jax.random.fold_in(jax.random.fold_in(key, 6), axis_at), (blocks,), jnp.float32, low / len(shards), top_value / len(shards))
        gain = gain * jnp.repeat(jnp.exp(steps), dims[axis_at] // blocks).reshape((-1,) + (1,) * (len(dims) - 1 - axis_at))
    return gain


def bell_draw(stream_key, shape, scale, reach, split=(), kind=jnp.bfloat16):
    array = scale * jax.random.normal(stream_key, shape, jnp.float32)
    if split:
        array = array * levels(stream_key, shape, split, -0.22, 0.18)
    return jnp.clip(array, -reach, reach).astype(kind)


def setup_inputs(seed: int = 0) -> dict:
    streams_of = jax.random.split(jax.random.key(seed), 3)
    return {
        "charges": bell_draw(streams_of[0], (REPLICAS * NG, NG, NZ), 1.0, 6.0, ((0, 64), (1, 8)), jnp.float32),
        "green": jnp.clip(jnp.exp(math.log(3.0) - 3.4011974 * jax.random.uniform(streams_of[1], (NG, NG, NZ), jnp.float32) ** levels(streams_of[1], (NG, NG, NZ), ((0, 16), (1, 32)), -0.2, 0.2)), 0.1, 3.0),
    }


def reference(charges, green):
    stacked = charges.reshape(REPLICAS, NG, NG, NZ)

    def single(charge):
        spectrum = jnp.fft.fftn(charge) * green
        return jnp.real(jnp.fft.ifftn(spectrum)).astype(jnp.float32)

    return lax.map(single, stacked).reshape(REPLICAS * NG, NG, NZ)
```

```python
import math

import jax
import jax.numpy as jnp
import ml_dtypes
import numpy as np
from jax import lax
from jax.experimental import pallas as pl
from jax.experimental.pallas import tpu as pltpu
from jax.sharding import PartitionSpec as P

NG = 256
NZ = 128
HALF = NZ // 2
GY = 8
GZ = 4
GROUP = GY * GZ
ROWS = NG // GZ
COLS = NG // GY
LANES = 128
LOW = LANES // COLS
HIGH = ROWS // LOW
CHUNK = 4

VMEM_LIMIT = 16 * 1024 * 1024
VMEM_ALL = 60 * 1024 * 1024
F32 = jnp.float32
BF16 = jnp.bfloat16


def parts_of(table, count=2):
    rest = np.asarray(table, np.float64)
    found = []
    for _ in range(count):
        piece = rest.astype(np.float32).astype(ml_dtypes.bfloat16)
        found.append(piece)
        rest = rest - piece.astype(np.float64)
    return found


def depth_tables():
    z = np.arange(NZ)
    there = np.zeros((2, 2, GROUP, NZ))
    back = np.zeros((2, 2, GROUP, NZ))
    for j in range(2):
        for s in range(GROUP):
            k = 2 * s + j
            angle = 2 * math.pi * ((k * z) % NZ) / NZ
            if k == 0:
                there[0, j, s] = 1.0
                there[1, j, s] = 1.0 - 2.0 * (z % 2)
                back[0, j, s] = 1.0
                back[1, j, s] = 2.0 * (z % 2) - 1.0
            else:
                there[0, j, s] = np.cos(angle)
                there[1, j, s] = -np.sin(angle)
                back[0, j, s] = 2 * np.cos(angle)
                back[1, j, s] = 2 * np.sin(angle)
    scale = 1.0 / (NG * NG * NZ)
    return there.reshape(4 * GROUP, NZ), back.reshape(4 * GROUP, NZ) * scale


def row_order():
    low, block, high = np.meshgrid(np.arange(LOW), np.arange(GZ), np.arange(HIGH), indexing="ij")
    return (block * ROWS + high * LOW + low).reshape(-1)


def plane_tables():
    index, order = np.arange(NG), row_order()
    angle = 2 * math.pi * (np.outer(index, index) % NG) / NG
    cos, sin = np.cos(angle), np.sin(angle)
    first = np.concatenate([cos[order][:, order], sin[order][:, order]], axis=1)
    return first, np.concatenate([cos, sin], axis=1)


def pick_table():
    pick = np.zeros((GROUP, 2, 2, NZ))
    for s in range(GROUP):
        for j in range(2):
            k = 2 * s + j
            pick[s, j, 0, k] = 1
            pick[s, j, 1, NZ // 2 if k == 0 else NZ - k] = 1
    return pick.reshape(4 * GROUP, NZ)


def gain_tables():
    index, order = np.arange(NG), row_order()
    place = (order[:, None] == index[None, :]).astype(np.float64)
    opposite = (index[:, None] == (-index[None, :]) % NG).astype(np.float64)
    return np.stack([place, place @ opposite, opposite])


def split2(x):
    high = x.astype(BF16)
    return high, (x - high.astype(F32)).astype(BF16)


def split3(x):
    high = x.astype(BF16)
    rest = x - high.astype(F32)
    mid = rest.astype(BF16)
    return high, mid, (rest - mid.astype(F32)).astype(BF16)


def dot(a, b, da=1, db=0):
    return lax.dot_general(a, b, (((da,), (db,)), ((), ())), preferred_element_type=F32)


def dot3(a, b, da=1, db=0):
    return dot(a[0], b[0], da, db) + (dot(a[0], b[1], da, db) + dot(a[1], b[0], da, db))


def swap_blocks(arrays):
    lane = lax.broadcasted_iota(jnp.int32, arrays[0].shape, 1)
    low_half = lane < 2 * COLS
    even = (lane // COLS) % 2 == 0

    def turn(x, by):
        return pltpu.roll(x, by % LANES, 1)

    x0, x1, x2, x3 = arrays
    y0 = jnp.where(low_half, x0, turn(x2, 2 * COLS))
    y2 = jnp.where(low_half, turn(x0, 2 * COLS), x2)
    y1 = jnp.where(low_half, x1, turn(x3, 2 * COLS))
    y3 = jnp.where(low_half, turn(x1, 2 * COLS), x3)
    z0 = jnp.where(even, y0, turn(y1, COLS))
    z1 = jnp.where(even, turn(y0, -COLS), y1)
    z2 = jnp.where(even, y2, turn(y3, COLS))
    z3 = jnp.where(even, turn(y2, -COLS), y3)
    return z0, z1, z2, z3


def fetch(sources, targets, sems):
    copies = [pltpu.make_async_copy(a, b, sems.at[i]) for i, (a, b) in enumerate(zip(sources, targets, strict=True))]
    for copy in copies:
        copy.start()
    return copies


def wait(copies):
    for copy in copies:
        copy.wait()


def depth_kernel(q_hbm, high_hbm, low_hbm, out_ref, q_ref, w_ref, sems):
    size = CHUNK * LANES
    tables = fetch((high_hbm, low_hbm), (w_ref.at[0], w_ref.at[1]), sems)
    copies = [
        pltpu.make_async_copy(q_hbm.at[i * size : (i + 1) * size], q_ref.at[i * size : (i + 1) * size], sems.at[2 + i])
        for i in range(HIGH // CHUNK)
    ]
    for copy in copies:
        copy.start()
    wait(tables)
    w = (w_ref[0], w_ref[1])
    for h in range(HIGH):
        if h % CHUNK == 0:
            copies[h // CHUNK].wait()
        q = split2(q_ref[h * LANES : (h + 1) * LANES, :])
        t = dot3(w, q, 1, 1)
        for c in range(4):
            out_ref[pl.ds(c * HIGH + h, GROUP, stride=ROWS), :] = t[c * GROUP : (c + 1) * GROUP, :]


def cells_kernel(r_ref, high_ref, low_ref, out_hbm, out_ref, sems):
    w = (high_ref[...], low_ref[...])
    size = CHUNK * LANES
    copies = []
    for h in range(HIGH):
        t = jnp.concatenate([r_ref[pl.ds(c * HIGH + h, GROUP, stride=ROWS), :] for c in range(4)], axis=0)
        out_ref[h * LANES : (h + 1) * LANES, :] = dot3(split2(t.T), w)
        if h % CHUNK == CHUNK - 1:
            i = h // CHUNK
            copies.append(
                pltpu.make_async_copy(out_ref.at[i * size : (i + 1) * size], out_hbm.at[i * size : (i + 1) * size], sems.at[i])
            )
            copies[-1].start()
    wait(copies)


def stacked(high_ref, low_ref, sign):
    def stack(t):
        cos, sin = t[:, :NG], t[:, NG:]
        rows = [[cos, sin], [-sin, cos]] if sign > 0 else [[cos, -sin], [sin, cos]]
        return jnp.concatenate([jnp.concatenate(row, axis=1) for row in rows], axis=0)

    return stack(high_ref[...]), stack(low_ref[...])


def there_kernel(r_ref, lh, ll, rh, rl, out_ref, p_ref):
    for part in range(2):
        for j in range(2):
            c = 2 * part + j
            for gh in range(GY // LOW):
                arrays = [
                    r_ref[(gh * LOW + g) * GZ : (gh * LOW + g + 1) * GZ, c * HIGH : (c + 1) * HIGH, :].reshape(ROWS, LANES)
                    for g in range(LOW)
                ]
                for a, value in enumerate(swap_blocks(arrays)):
                    row, col = part * NG + a * ROWS, j * NG + gh * LANES
                    p_ref[row : row + ROWS, col : col + LANES] = value
    y = dot3(stacked(lh, ll, 1), split2(p_ref[...]))
    y = [jnp.concatenate([y[:NG, j * NG : (j + 1) * NG], y[NG:, j * NG : (j + 1) * NG]], axis=1) for j in range(2)]
    out_ref[...] = dot3(split2(jnp.concatenate(y, axis=0)), stacked(rh, rl, -1))


def back_kernel(f_ref, gain_ref, lh, ll, rh, rl, out_ref):
    columns = []
    for p in range(3):
        rows = slice(p // 2 * NG, (p // 2 + 1) * NG)
        gain = gain_ref[p]
        columns.append(jnp.concatenate([f_ref[rows, :NG] * gain, f_ref[rows, NG:] * -gain], axis=0))
    u = dot3(stacked(lh, ll, 1), split2(jnp.concatenate(columns, axis=1)))
    u = [split2(jnp.concatenate([u[:NG, p * NG : (p + 1) * NG], u[NG:, p * NG : (p + 1) * NG]], axis=1)) for p in range(3)]
    right = stacked(rh, rl, -1)
    v = {(0, 0): dot3(u[0], tuple(t[:, :NG] for t in right)), (1, 0): dot3(u[1], tuple(t[:, NG:] for t in right))}
    both = dot3(u[2], right)
    v[0, 1], v[1, 1] = both[:, :NG], both[:, NG:]
    for (part, j), value in v.items():
        c = 2 * part + j
        for gh in range(GY // LOW):
            arrays = [value[a * ROWS : (a + 1) * ROWS, gh * LANES : (gh + 1) * LANES] for a in range(LOW)]
            for g, cells in enumerate(swap_blocks(arrays)):
                out_ref[(gh * LOW + g) * GZ : (gh * LOW + g + 1) * GZ, c * HIGH : (c + 1) * HIGH, :] = cells.reshape(GZ, HIGH, LANES)


def pick_kernel(g_hbm, pick_hbm, out_ref, g_ref, pick_ref, sems):
    wait(fetch((g_hbm, pick_hbm), (g_ref, pick_ref), sems))
    pick = pick_ref[...]
    chosen = sum(dot(pick, piece, 1, 1) for piece in split3(g_ref[...]))
    for t in range(2):
        out_ref[t * 4 * GROUP : (t + 1) * 4 * GROUP, :] = chosen


def lay_kernel(g_ref, out_ref):
    deep = g_ref.shape[1] // 8
    grow_row = lax.broadcasted_iota(jnp.int32, (GROUP, NG), 0)
    grow_col = lax.broadcasted_iota(jnp.int32, (GROUP, NG), 1)
    grow = (grow_row == grow_col // 8).astype(F32).astype(BF16)
    keep_row = lax.broadcasted_iota(jnp.int32, (deep * 8, NG), 0)
    keep_col = lax.broadcasted_iota(jnp.int32, (deep * 8, NG), 1)
    keep = keep_row % 8 == keep_col % 8
    for t in range(2):
        for p in range(4):
            rows = g_ref[pl.ds(t * 4 * GROUP + p, GROUP, stride=4), :].T
            wide = sum(dot(piece, grow) for piece in split3(rows))
            wide = jnp.where(keep, wide, 0.0)
            out_ref[t, p] = jnp.sum(wide.reshape(deep, 8, NG), axis=1)


def gain_kernel(where_ref, *refs):
    *pieces, table_ref, out_ref, all_ref = refs
    depth, slot = where_ref[0], where_ref[1]
    count = len(pieces)
    deep = NG // (2 * count)
    for step, piece in enumerate(pieces):
        shift = step if step <= count // 2 else step - count
        owner = lax.rem(depth - shift + count, count)
        for t in range(2):
            at = (owner * 2 + t) * deep
            for p in range(4):
                all_ref[p, pl.ds(pl.multiple_of(at, 8), deep), :] = piece[t, p]
    place, opposite_rows, opposite = table_ref[0], table_ref[1], table_ref[2]

    def placed(x):
        return sum(dot(place, piece) for piece in split3(x))

    def reflected(x):
        x = sum(dot(opposite_rows, piece) for piece in split3(x))
        return sum(dot(piece, opposite) for piece in split3(x))

    packed = slot == 0
    own, other = all_ref[0], all_ref[1]
    out_ref[0] = 0.5 * (placed(own) + reflected(jnp.where(packed, own, other)))
    out_ref[1] = 0.5 * (placed(jnp.where(packed, other, own)) + reflected(other))
    out_ref[2] = 0.5 * (placed(all_ref[2]) + reflected(all_ref[3]))


def call(kernel, out_shape, operands, name, flops=0, scratch=(), spaces=None, out_space=pltpu.VMEM, vmem=VMEM_LIMIT):
    moved = sum(x.size * x.dtype.itemsize for x in operands) + math.prod(out_shape) * 4
    spaces = spaces or [pltpu.VMEM] * len(operands)
    return pl.pallas_call(
        kernel,
        out_shape=jax.ShapeDtypeStruct(out_shape, F32),
        in_specs=[pl.BlockSpec(memory_space=space) for space in spaces],
        out_specs=pl.BlockSpec(memory_space=out_space),
        scratch_shapes=list(scratch),
        compiler_params=pltpu.CompilerParams(vmem_limit_bytes=vmem),
        cost_estimate=pl.CostEstimate(flops=flops, bytes_accessed=moved, transcendentals=0),
        name=name,
    )(*operands)


def gains(green):
    depth_count = lax.axis_size("z")
    deep = green.shape[0]
    slot = lax.axis_index("gy") * GZ + lax.axis_index("gz")
    pick = jnp.asarray(pick_table().astype(ml_dtypes.bfloat16))
    sent = call(
        pick_kernel,
        (2 * 4 * GROUP, deep * 8),
        (green.reshape(deep * 8, NZ), pick),
        "pick",
        flops=6 * 128**3,
        spaces=[pltpu.HBM] * 2,
        vmem=VMEM_ALL,
        scratch=[pltpu.VMEM((deep * 8, NZ), F32), pltpu.VMEM((4 * GROUP, NZ), BF16), pltpu.SemaphoreType.DMA((2,))],
    )
    sent = sent.reshape(2 * GROUP, 4, deep * 8)
    got = lax.all_to_all(sent, ("y_lo", "gy", "gz"), split_axis=0, concat_axis=0, tiled=True)
    pair = call(lay_kernel, (2, 4, deep, NG), (got.reshape(2 * 4 * GROUP, deep * 8),), "lay", flops=48 * 128 * 32 * 256)
    def along(value, by):
        return lax.ppermute(value, "z", [(i, (i + by) % depth_count) for i in range(depth_count)])

    from_ = {0: pair, 1: along(pair, 1), -1: along(pair, -1), 2: along(pair, 2), -2: along(pair, -2)}
    from_[3] = along(from_[1], 2)
    from_[-3] = along(from_[-1], -2)
    from_[4] = along(from_[2], 2)
    pieces = [from_[k] for k in (0, 1, 2, 3, 4, -3, -2, -1)]
    where = jnp.stack([lax.axis_index("z"), slot]).astype(jnp.int32)
    selections = jnp.asarray(gain_tables().astype(ml_dtypes.bfloat16))
    return call(
        gain_kernel,
        (3, NG, NG),
        (where, *pieces, selections),
        "gain",
        flops=54 * NG**3,
        scratch=[pltpu.VMEM((4, NG, NG), F32)],
        spaces=[pltpu.SMEM] + [pltpu.VMEM] * 9,
    )


def on_device(charges, green):
    there, back = depth_tables()
    there = [jnp.asarray(t) for t in parts_of(there)]
    back = [jnp.asarray(t) for t in parts_of(back)]
    tables = [jnp.asarray(t) for table in plane_tables() for t in parts_of(table)]
    gain = gains(green)
    cells = ROWS * COLS
    chunks = HIGH // CHUNK
    sent = call(
        depth_kernel,
        (GROUP * ROWS, LANES),
        (charges.reshape(cells, NZ), *there),
        "depth",
        flops=6 * cells * NZ * NZ,
        spaces=[pltpu.HBM] * 3,
        vmem=VMEM_ALL,
        scratch=[pltpu.VMEM((cells, NZ), F32), pltpu.VMEM((2, 4 * GROUP, NZ), BF16), pltpu.SemaphoreType.DMA((2 + chunks,))],
    )
    sent = sent.reshape(GROUP, ROWS, LANES)
    got = lax.all_to_all(sent, ("gy", "gz"), split_axis=0, concat_axis=0, tiled=True)
    spectra = call(
        there_kernel,
        (2 * NG, 2 * NG),
        (got, *tables),
        "there",
        flops=6 * 16 * NG**3,
        scratch=[pltpu.VMEM((2 * NG, 2 * NG), F32)],
    )
    sent = call(
        back_kernel,
        (GROUP, ROWS, LANES),
        (spectra, gain, *tables),
        "back",
        flops=6 * 20 * NG**3,
    )
    got = lax.all_to_all(sent, ("gy", "gz"), split_axis=0, concat_axis=0, tiled=True)
    out = call(
        cells_kernel,
        (cells, NZ),
        (got.reshape(GROUP * ROWS, LANES), *back),
        "cells",
        flops=6 * cells * NZ * NZ,
        scratch=[pltpu.VMEM((cells, NZ), F32), pltpu.SemaphoreType.DMA((chunks,))],
        out_space=pltpu.HBM,
    )
    return out.reshape(charges.shape)


def solution(mesh):
    apart = jax.sharding.Mesh(
        mesh.devices.reshape(mesh.shape["rep"] // 2, 2, mesh.shape["gy"], mesh.shape["gz"]), ("z", "y_lo", "gy", "gz")
    )
    return jax.shard_map(
        on_device,
        mesh=apart,
        in_specs=(P(("z", "y_lo", "gz"), "gy", None), P(("z", "y_lo"), ("gy", "gz"), None)),
        out_specs=P(("z", "y_lo", "gz"), "gy", None),
        check_vma=False,
    )
```

```python
import math

import jax
import jax.numpy as jnp
import ml_dtypes
import numpy as np
from jax import lax
from jax.experimental import pallas as pl
from jax.experimental.pallas import tpu as pltpu
from jax.sharding import PartitionSpec as P

NG = 256
NZ = 128
HALF = NZ // 2
GY = 8
GZ = 4
GROUP = GY * GZ
ROWS = NG // GZ
COLS = NG // GY
LANES = 128
LOW = LANES // COLS
HIGH = ROWS // LOW
CHUNK = 4

VMEM_LIMIT = 16 * 1024 * 1024
VMEM_ALL = 60 * 1024 * 1024
F32 = jnp.float32
BF16 = jnp.bfloat16


def parts_of(table, count=2):
    rest = np.asarray(table, np.float64)
    found = []
    for _ in range(count):
        piece = rest.astype(np.float32).astype(ml_dtypes.bfloat16)
        found.append(piece)
        rest = rest - piece.astype(np.float64)
    return found


def depth_tables():
    z = np.arange(NZ)
    there = np.zeros((2, 2, GROUP, NZ))
    back = np.zeros((2, 2, GROUP, NZ))
    for j in range(2):
        for s in range(GROUP):
            k = 2 * s + j
            angle = 2 * math.pi * ((k * z) % NZ) / NZ
            if k == 0:
                there[0, j, s] = 1.0
                there[1, j, s] = 1.0 - 2.0 * (z % 2)
                back[0, j, s] = 1.0
                back[1, j, s] = 2.0 * (z % 2) - 1.0
            else:
                there[0, j, s] = np.cos(angle)
                there[1, j, s] = -np.sin(angle)
                back[0, j, s] = 2 * np.cos(angle)
                back[1, j, s] = 2 * np.sin(angle)
    scale = 1.0 / (NG * NG * NZ)
    return there.reshape(4 * GROUP, NZ), back.reshape(4 * GROUP, NZ) * scale


def row_order():
    low, block, high = np.meshgrid(np.arange(LOW), np.arange(GZ), np.arange(HIGH), indexing="ij")
    return (block * ROWS + high * LOW + low).reshape(-1)


def plane_tables():
    index, order = np.arange(NG), row_order()
    angle = 2 * math.pi * (np.outer(index, index) % NG) / NG
    cos, sin = np.cos(angle), np.sin(angle)
    first = np.concatenate([cos[order][:, order], sin[order][:, order]], axis=1)
    return first, np.concatenate([cos, sin], axis=1)


def pick_table():
    pick = np.zeros((GROUP, 2, 2, NZ))
    for s in range(GROUP):
        for j in range(2):
            k = 2 * s + j
            pick[s, j, 0, k] = 1
            pick[s, j, 1, NZ // 2 if k == 0 else NZ - k] = 1
    return pick.reshape(4 * GROUP, NZ)


def gain_tables():
    index, order = np.arange(NG), row_order()
    place = (order[:, None] == index[None, :]).astype(np.float64)
    opposite = (index[:, None] == (-index[None, :]) % NG).astype(np.float64)
    return np.stack([place, place @ opposite, opposite])


def split2(x):
    high = x.astype(BF16)
    return high, (x - high.astype(F32)).astype(BF16)


def split3(x):
    high = x.astype(BF16)
    rest = x - high.astype(F32)
    mid = rest.astype(BF16)
    return high, mid, (rest - mid.astype(F32)).astype(BF16)


def dot(a, b, da=1, db=0):
    return lax.dot_general(a, b, (((da,), (db,)), ((), ())), preferred_element_type=F32)


def dot3(a, b, da=1, db=0):
    return dot(a[0], b[0], da, db) + (dot(a[0], b[1], da, db) + dot(a[1], b[0], da, db))


def swap_blocks(arrays):
    lane = lax.broadcasted_iota(jnp.int32, arrays[0].shape, 1)
    low_half = lane < 2 * COLS
    even = (lane // COLS) % 2 == 0

    def turn(x, by):
        return pltpu.roll(x, by % LANES, 1)

    x0, x1, x2, x3 = arrays
    y0 = jnp.where(low_half, x0, turn(x2, 2 * COLS))
    y2 = jnp.where(low_half, turn(x0, 2 * COLS), x2)
    y1 = jnp.where(low_half, x1, turn(x3, 2 * COLS))
    y3 = jnp.where(low_half, turn(x1, 2 * COLS), x3)
    z0 = jnp.where(even, y0, turn(y1, COLS))
    z1 = jnp.where(even, turn(y0, -COLS), y1)
    z2 = jnp.where(even, y2, turn(y3, COLS))
    z3 = jnp.where(even, turn(y2, -COLS), y3)
    return z0, z1, z2, z3


def fetch(sources, targets, sems):
    copies = [pltpu.make_async_copy(a, b, sems.at[i]) for i, (a, b) in enumerate(zip(sources, targets, strict=True))]
    for copy in copies:
        copy.start()
    return copies


def wait(copies):
    for copy in copies:
        copy.wait()


def depth_kernel(q_hbm, high_hbm, low_hbm, out_ref, q_ref, w_ref, sems):
    size = CHUNK * LANES
    tables = fetch((high_hbm, low_hbm), (w_ref.at[0], w_ref.at[1]), sems)
    copies = [
        pltpu.make_async_copy(q_hbm.at[i * size : (i + 1) * size], q_ref.at[i * size : (i + 1) * size], sems.at[2 + i])
        for i in range(HIGH // CHUNK)
    ]
    for copy in copies:
        copy.start()
    wait(tables)
    w = (w_ref[0], w_ref[1])
    for h in range(HIGH):
        if h % CHUNK == 0:
            copies[h // CHUNK].wait()
        q = split2(q_ref[h * LANES : (h + 1) * LANES, :])
        t = dot3(w, q, 1, 1)
        for c in range(4):
            out_ref[pl.ds(c * HIGH + h, GROUP, stride=ROWS), :] = t[c * GROUP : (c + 1) * GROUP, :]


def cells_kernel(r_ref, high_ref, low_ref, out_hbm, out_ref, sems):
    w = (high_ref[...], low_ref[...])
    size = CHUNK * LANES
    copies = []
    for h in range(HIGH):
        t = jnp.concatenate([r_ref[pl.ds(c * HIGH + h, GROUP, stride=ROWS), :] for c in range(4)], axis=0)
        out_ref[h * LANES : (h + 1) * LANES, :] = dot3(split2(t.T), w)
        if h % CHUNK == CHUNK - 1:
            i = h // CHUNK
            copies.append(
                pltpu.make_async_copy(out_ref.at[i * size : (i + 1) * size], out_hbm.at[i * size : (i + 1) * size], sems.at[i])
            )
            copies[-1].start()
    wait(copies)


def stacked(high_ref, low_ref, sign):
    def stack(t):
        cos, sin = t[:, :NG], t[:, NG:]
        rows = [[cos, sin], [-sin, cos]] if sign > 0 else [[cos, -sin], [sin, cos]]
        return jnp.concatenate([jnp.concatenate(row, axis=1) for row in rows], axis=0)

    return stack(high_ref[...]), stack(low_ref[...])


def there_kernel(r_ref, lh, ll, rh, rl, out_ref, p_ref):
    for part in range(2):
        for j in range(2):
            c = 2 * part + j
            for gh in range(GY // LOW):
                arrays = [
                    r_ref[(gh * LOW + g) * GZ : (gh * LOW + g + 1) * GZ, c * HIGH : (c + 1) * HIGH, :].reshape(ROWS, LANES)
                    for g in range(LOW)
                ]
                for a, value in enumerate(swap_blocks(arrays)):
                    row, col = part * NG + a * ROWS, j * NG + gh * LANES
                    p_ref[row : row + ROWS, col : col + LANES] = value
    y = dot3(stacked(lh, ll, 1), split2(p_ref[...]))
    y = [jnp.concatenate([y[:NG, j * NG : (j + 1) * NG], y[NG:, j * NG : (j + 1) * NG]], axis=1) for j in range(2)]
    out_ref[...] = dot3(split2(jnp.concatenate(y, axis=0)), stacked(rh, rl, -1))


def back_kernel(f_ref, gain_ref, lh, ll, rh, rl, out_ref):
    columns = []
    for p in range(3):
        rows = slice(p // 2 * NG, (p // 2 + 1) * NG)
        gain = gain_ref[p]
        columns.append(jnp.concatenate([f_ref[rows, :NG] * gain, f_ref[rows, NG:] * -gain], axis=0))
    u = dot3(stacked(lh, ll, 1), split2(jnp.concatenate(columns, axis=1)))
    u = [split2(jnp.concatenate([u[:NG, p * NG : (p + 1) * NG], u[NG:, p * NG : (p + 1) * NG]], axis=1)) for p in range(3)]
    right = stacked(rh, rl, -1)
    v = {(0, 0): dot3(u[0], tuple(t[:, :NG] for t in right)), (1, 0): dot3(u[1], tuple(t[:, NG:] for t in right))}
    both = dot3(u[2], right)
    v[0, 1], v[1, 1] = both[:, :NG], both[:, NG:]
    for (part, j), value in v.items():
        c = 2 * part + j
        for gh in range(GY // LOW):
            arrays = [value[a * ROWS : (a + 1) * ROWS, gh * LANES : (gh + 1) * LANES] for a in range(LOW)]
            for g, cells in enumerate(swap_blocks(arrays)):
                out_ref[(gh * LOW + g) * GZ : (gh * LOW + g + 1) * GZ, c * HIGH : (c + 1) * HIGH, :] = cells.reshape(GZ, HIGH, LANES)


def pick_kernel(g_hbm, pick_hbm, out_ref, g_ref, pick_ref, sems):
    wait(fetch((g_hbm, pick_hbm), (g_ref, pick_ref), sems))
    pick = pick_ref[...]
    chosen = sum(dot(pick, piece, 1, 1) for piece in split3(g_ref[...]))
    for t in range(2):
        out_ref[t * 4 * GROUP : (t + 1) * 4 * GROUP, :] = chosen


def lay_kernel(g_ref, out_ref):
    deep = g_ref.shape[1] // 8
    grow_row = lax.broadcasted_iota(jnp.int32, (GROUP, NG), 0)
    grow_col = lax.broadcasted_iota(jnp.int32, (GROUP, NG), 1)
    grow = (grow_row == grow_col // 8).astype(F32).astype(BF16)
    keep_row = lax.broadcasted_iota(jnp.int32, (deep * 8, NG), 0)
    keep_col = lax.broadcasted_iota(jnp.int32, (deep * 8, NG), 1)
    keep = keep_row % 8 == keep_col % 8
    for t in range(2):
        for p in range(4):
            rows = g_ref[pl.ds(t * 4 * GROUP + p, GROUP, stride=4), :].T
            wide = sum(dot(piece, grow) for piece in split3(rows))
            wide = jnp.where(keep, wide, 0.0)
            out_ref[t, p] = jnp.sum(wide.reshape(deep, 8, NG), axis=1)


def gain_kernel(where_ref, *refs):
    *pieces, table_ref, out_ref, all_ref = refs
    depth, slot = where_ref[0], where_ref[1]
    count = len(pieces)
    deep = NG // (2 * count)
    for step, piece in enumerate(pieces):
        shift = step if step <= count // 2 else step - count
        owner = lax.rem(depth - shift + count, count)
        for t in range(2):
            at = (owner * 2 + t) * deep
            for p in range(4):
                all_ref[p, pl.ds(pl.multiple_of(at, 8), deep), :] = piece[t, p]
    place, opposite_rows, opposite = table_ref[0], table_ref[1], table_ref[2]

    def placed(x):
        return sum(dot(place, piece) for piece in split2(x))

    def reflected(x):
        x = sum(dot(opposite_rows, piece) for piece in split2(x))
        return sum(dot(piece, opposite) for piece in split2(x))

    packed = slot == 0
    own, other = all_ref[0], all_ref[1]
    out_ref[0] = 0.5 * (placed(own) + reflected(jnp.where(packed, own, other)))
    out_ref[1] = 0.5 * (placed(jnp.where(packed, other, own)) + reflected(other))
    out_ref[2] = 0.5 * (placed(all_ref[2]) + reflected(all_ref[3]))


def call(kernel, out_shape, operands, name, flops=0, scratch=(), spaces=None, out_space=pltpu.VMEM, vmem=VMEM_LIMIT):
    moved = sum(x.size * x.dtype.itemsize for x in operands) + math.prod(out_shape) * 4
    spaces = spaces or [pltpu.VMEM] * len(operands)
    return pl.pallas_call(
        kernel,
        out_shape=jax.ShapeDtypeStruct(out_shape, F32),
        in_specs=[pl.BlockSpec(memory_space=space) for space in spaces],
        out_specs=pl.BlockSpec(memory_space=out_space),
        scratch_shapes=list(scratch),
        compiler_params=pltpu.CompilerParams(vmem_limit_bytes=vmem),
        cost_estimate=pl.CostEstimate(flops=flops, bytes_accessed=moved, transcendentals=0),
        name=name,
    )(*operands)


def spread(green):
    depth_count = lax.axis_size("z")
    deep = green.shape[0]
    pick = jnp.asarray(pick_table().astype(ml_dtypes.bfloat16))
    sent = call(
        pick_kernel,
        (2 * 4 * GROUP, deep * 8),
        (green.reshape(deep * 8, NZ), pick),
        "pick",
        flops=6 * 128**3,
        spaces=[pltpu.HBM] * 2,
        vmem=VMEM_ALL,
        scratch=[pltpu.VMEM((deep * 8, NZ), F32), pltpu.VMEM((4 * GROUP, NZ), BF16), pltpu.SemaphoreType.DMA((2,))],
    )
    sent = sent.reshape(2 * GROUP, 4, deep * 8)
    got = lax.all_to_all(sent, ("y_lo", "gy", "gz"), split_axis=0, concat_axis=0, tiled=True)
    pair = call(lay_kernel, (2, 4, deep, NG), (got.reshape(2 * 4 * GROUP, deep * 8),), "lay", flops=48 * 128 * 32 * 256)
    def along(value, by):
        return lax.ppermute(value, "z", [(i, (i + by) % depth_count) for i in range(depth_count)])

    from_ = {0: pair, 1: along(pair, 1), -1: along(pair, -1), 2: along(pair, 2), -2: along(pair, -2)}
    from_[3] = along(from_[1], 2)
    from_[-3] = along(from_[-1], -2)
    from_[4] = along(from_[2], 2)
    pieces = [from_[k] for k in (0, 1, 2, 3, 4, -3, -2, -1)]
    return pieces


def gains(pieces):
    slot = lax.axis_index("gy") * GZ + lax.axis_index("gz")
    where = jnp.stack([lax.axis_index("z"), slot]).astype(jnp.int32)
    selections = jnp.asarray(gain_tables().astype(ml_dtypes.bfloat16))
    return call(
        gain_kernel,
        (3, NG, NG),
        (where, *pieces, selections),
        "gain",
        flops=54 * NG**3,
        scratch=[pltpu.VMEM((4, NG, NG), F32)],
        spaces=[pltpu.SMEM] + [pltpu.VMEM] * 9,
    )


def on_device(charges, green):
    there, back = depth_tables()
    there = [jnp.asarray(t) for t in parts_of(there)]
    back = [jnp.asarray(t) for t in parts_of(back)]
    tables = [jnp.asarray(t) for table in plane_tables() for t in parts_of(table)]
    pieces = spread(green)
    cells = ROWS * COLS
    chunks = HIGH // CHUNK
    sent = call(
        depth_kernel,
        (GROUP * ROWS, LANES),
        (charges.reshape(cells, NZ), *there),
        "depth",
        flops=6 * cells * NZ * NZ,
        spaces=[pltpu.HBM] * 3,
        vmem=VMEM_ALL,
        scratch=[pltpu.VMEM((cells, NZ), F32), pltpu.VMEM((2, 4 * GROUP, NZ), BF16), pltpu.SemaphoreType.DMA((2 + chunks,))],
    )
    sent = sent.reshape(GROUP, ROWS, LANES)
    got = lax.all_to_all(sent, ("gy", "gz"), split_axis=0, concat_axis=0, tiled=True)
    spectra = call(
        there_kernel,
        (2 * NG, 2 * NG),
        (got, *tables),
        "there",
        flops=6 * 16 * NG**3,
        scratch=[pltpu.VMEM((2 * NG, 2 * NG), F32)],
    )
    spectra, *pieces[3:6] = lax.optimization_barrier((spectra, *pieces[3:6]))
    sent = call(
        back_kernel,
        (GROUP, ROWS, LANES),
        (spectra, gains(pieces), *tables),
        "back",
        flops=6 * 20 * NG**3,
    )
    got = lax.all_to_all(sent, ("gy", "gz"), split_axis=0, concat_axis=0, tiled=True)
    out = call(
        cells_kernel,
        (cells, NZ),
        (got.reshape(GROUP * ROWS, LANES), *back),
        "cells",
        flops=6 * cells * NZ * NZ,
        scratch=[pltpu.VMEM((cells, NZ), F32), pltpu.SemaphoreType.DMA((chunks,))],
        out_space=pltpu.HBM,
    )
    return out.reshape(charges.shape)


def solution(mesh):
    apart = jax.sharding.Mesh(
        mesh.devices.reshape(mesh.shape["rep"] // 2, 2, mesh.shape["gy"], mesh.shape["gz"]), ("z", "y_lo", "gy", "gz")
    )
    return jax.shard_map(
        on_device,
        mesh=apart,
        in_specs=(P(("z", "y_lo", "gz"), "gy", None), P(("z", "y_lo"), ("gy", "gz"), None)),
        out_specs=P(("z", "y_lo", "gz"), "gy", None),
        check_vma=False,
    )
```

```python
import math

import jax
import jax.numpy as jnp
import ml_dtypes
import numpy as np
from jax import lax
from jax.experimental import pallas as pl
from jax.experimental.pallas import tpu as pltpu
from jax.sharding import PartitionSpec as P

NG = 256
NZ = 128
HALF = NZ // 2
GY = 8
GZ = 4
GROUP = GY * GZ
ROWS = NG // GZ
COLS = NG // GY
LANES = 128
LOW = LANES // COLS
HIGH = ROWS // LOW
CHUNK = 4

VMEM_LIMIT = 16 * 1024 * 1024
VMEM_ALL = 60 * 1024 * 1024
F32 = jnp.float32
BF16 = jnp.bfloat16


def parts_of(table, count=2):
    rest = np.asarray(table, np.float64)
    found = []
    for _ in range(count):
        piece = rest.astype(np.float32).astype(ml_dtypes.bfloat16)
        found.append(piece)
        rest = rest - piece.astype(np.float64)
    return found


def depth_tables():
    z = np.arange(NZ)
    there = np.zeros((2, 2, GROUP, NZ))
    back = np.zeros((2, 2, GROUP, NZ))
    for j in range(2):
        for s in range(GROUP):
            k = 2 * s + j
            angle = 2 * math.pi * ((k * z) % NZ) / NZ
            if k == 0:
                there[0, j, s] = 1.0
                there[1, j, s] = 1.0 - 2.0 * (z % 2)
                back[0, j, s] = 1.0
                back[1, j, s] = 2.0 * (z % 2) - 1.0
            else:
                there[0, j, s] = np.cos(angle)
                there[1, j, s] = -np.sin(angle)
                back[0, j, s] = 2 * np.cos(angle)
                back[1, j, s] = 2 * np.sin(angle)
    scale = 1.0 / (NG * NG * NZ)
    return there.reshape(4 * GROUP, NZ), back.reshape(4 * GROUP, NZ) * scale


def row_order():
    low, block, high = np.meshgrid(np.arange(LOW), np.arange(GZ), np.arange(HIGH), indexing="ij")
    return (block * ROWS + high * LOW + low).reshape(-1)


def plane_tables():
    index, order = np.arange(NG), row_order()
    angle = 2 * math.pi * (np.outer(index, index) % NG) / NG
    cos, sin = np.cos(angle), np.sin(angle)
    first = np.concatenate([cos[order][:, order], sin[order][:, order]], axis=1)
    return first, np.concatenate([cos, sin], axis=1)


def pick_table():
    pick = np.zeros((GROUP, 2, 2, NZ))
    for s in range(GROUP):
        for j in range(2):
            k = 2 * s + j
            pick[s, j, 0, k] = 1
            pick[s, j, 1, NZ // 2 if k == 0 else NZ - k] = 1
    return pick.reshape(4 * GROUP, NZ)


def gain_tables():
    index, order = np.arange(NG), row_order()
    place = (order[:, None] == index[None, :]).astype(np.float64)
    opposite = (index[:, None] == (-index[None, :]) % NG).astype(np.float64)
    return np.stack([place, place @ opposite, opposite])


def split2(x):
    high = x.astype(BF16)
    return high, (x - high.astype(F32)).astype(BF16)


def split3(x):
    high = x.astype(BF16)
    rest = x - high.astype(F32)
    mid = rest.astype(BF16)
    return high, mid, (rest - mid.astype(F32)).astype(BF16)


def dot(a, b, da=1, db=0):
    return lax.dot_general(a, b, (((da,), (db,)), ((), ())), preferred_element_type=F32)


def dot3(a, b, da=1, db=0):
    return dot(a[0], b[0], da, db) + (dot(a[0], b[1], da, db) + dot(a[1], b[0], da, db))


def swap_blocks(arrays):
    lane = lax.broadcasted_iota(jnp.int32, arrays[0].shape, 1)
    low_half = lane < 2 * COLS
    even = (lane // COLS) % 2 == 0

    def turn(x, by):
        return pltpu.roll(x, by % LANES, 1)

    x0, x1, x2, x3 = arrays
    y0 = jnp.where(low_half, x0, turn(x2, 2 * COLS))
    y2 = jnp.where(low_half, turn(x0, 2 * COLS), x2)
    y1 = jnp.where(low_half, x1, turn(x3, 2 * COLS))
    y3 = jnp.where(low_half, turn(x1, 2 * COLS), x3)
    z0 = jnp.where(even, y0, turn(y1, COLS))
    z1 = jnp.where(even, turn(y0, -COLS), y1)
    z2 = jnp.where(even, y2, turn(y3, COLS))
    z3 = jnp.where(even, turn(y2, -COLS), y3)
    return z0, z1, z2, z3


def fetch(sources, targets, sems):
    copies = [pltpu.make_async_copy(a, b, sems.at[i]) for i, (a, b) in enumerate(zip(sources, targets, strict=True))]
    for copy in copies:
        copy.start()
    return copies


def wait(copies):
    for copy in copies:
        copy.wait()


def depth_kernel(q_hbm, high_hbm, low_hbm, out_ref, q_ref, w_ref, sems):
    size = CHUNK * LANES
    tables = fetch((high_hbm, low_hbm), (w_ref.at[0], w_ref.at[1]), sems)
    copies = [
        pltpu.make_async_copy(q_hbm.at[i * size : (i + 1) * size], q_ref.at[i * size : (i + 1) * size], sems.at[2 + i])
        for i in range(HIGH // CHUNK)
    ]
    for copy in copies:
        copy.start()
    wait(tables)
    w = (w_ref[0], w_ref[1])
    for h in range(HIGH):
        if h % CHUNK == 0:
            copies[h // CHUNK].wait()
        q = split2(q_ref[h * LANES : (h + 1) * LANES, :])
        t = dot3(w, q, 1, 1)
        for c in range(4):
            out_ref[pl.ds(c * HIGH + h, GROUP, stride=ROWS), :] = t[c * GROUP : (c + 1) * GROUP, :]


def cells_kernel(r_ref, high_ref, low_ref, out_hbm, out_ref, sems):
    w = (high_ref[...], low_ref[...])
    size = CHUNK * LANES
    copies = []
    for h in range(HIGH):
        t = jnp.concatenate([r_ref[pl.ds(c * HIGH + h, GROUP, stride=ROWS), :] for c in range(4)], axis=0)
        out_ref[h * LANES : (h + 1) * LANES, :] = dot3(split2(t.T), w)
        if h % CHUNK == CHUNK - 1:
            i = h // CHUNK
            copies.append(
                pltpu.make_async_copy(out_ref.at[i * size : (i + 1) * size], out_hbm.at[i * size : (i + 1) * size], sems.at[i])
            )
            copies[-1].start()
    wait(copies)


def stacked(high_ref, low_ref, sign):
    def stack(t):
        cos, sin = t[:, :NG], t[:, NG:]
        rows = [[cos, sin], [-sin, cos]] if sign > 0 else [[cos, -sin], [sin, cos]]
        return jnp.concatenate([jnp.concatenate(row, axis=1) for row in rows], axis=0)

    return stack(high_ref[...]), stack(low_ref[...])


def there_kernel(r_ref, lh, ll, rh, rl, out_ref, p_ref):
    for part in range(2):
        for j in range(2):
            c = 2 * part + j
            for gh in range(GY // LOW):
                arrays = [
                    r_ref[(gh * LOW + g) * GZ : (gh * LOW + g + 1) * GZ, c * HIGH : (c + 1) * HIGH, :].reshape(ROWS, LANES)
                    for g in range(LOW)
                ]
                for a, value in enumerate(swap_blocks(arrays)):
                    row, col = part * NG + a * ROWS, j * NG + gh * LANES
                    p_ref[row : row + ROWS, col : col + LANES] = value
    y = dot3(stacked(lh, ll, 1), split2(p_ref[...]))
    y = [jnp.concatenate([y[:NG, j * NG : (j + 1) * NG], y[NG:, j * NG : (j + 1) * NG]], axis=1) for j in range(2)]
    out_ref[...] = dot3(split2(jnp.concatenate(y, axis=0)), stacked(rh, rl, -1))


def across(t):
    return jnp.concatenate([t[0], t[0], t[1]], axis=1)


def down(t):
    return jnp.concatenate([t[0], t[1], t[0]], axis=0)


def back_kernel(where_ref, f_ref, early_ref, *refs):
    *halves, table_ref, lh, ll, rh, rl, out_ref, rows_ref, late_ref = refs
    columns = []
    for p, gain in enumerate(late_gains(where_ref, halves, early_ref, table_ref, rows_ref, late_ref)):
        rows = slice(p // 2 * NG, (p // 2 + 1) * NG)
        columns.append(jnp.concatenate([f_ref[rows, :NG] * gain, f_ref[rows, NG:] * -gain], axis=0))
    u = dot(across(stacked(lh, ll, 1)), down(split2(jnp.concatenate(columns, axis=1))))
    u = [split2(jnp.concatenate([u[:NG, p * NG : (p + 1) * NG], u[NG:, p * NG : (p + 1) * NG]], axis=1)) for p in range(3)]
    u = [across(t) for t in u]
    right = down(stacked(rh, rl, -1))
    v = {(0, 0): dot(u[0], right[:, :NG]), (1, 0): dot(u[1], right[:, NG:])}
    both = dot(u[2], right)
    v[0, 1], v[1, 1] = both[:, :NG], both[:, NG:]
    for (part, j), value in v.items():
        c = 2 * part + j
        for gh in range(GY // LOW):
            arrays = [value[a * ROWS : (a + 1) * ROWS, gh * LANES : (gh + 1) * LANES] for a in range(LOW)]
            for g, cells in enumerate(swap_blocks(arrays)):
                out_ref[(gh * LOW + g) * GZ : (gh * LOW + g + 1) * GZ, c * HIGH : (c + 1) * HIGH, :] = cells.reshape(GZ, HIGH, LANES)


def pick_kernel(g_hbm, pick_hbm, out_ref, g_ref, pick_ref, sems):
    wait(fetch((g_hbm, pick_hbm), (g_ref, pick_ref), sems))
    pick = pick_ref[...]
    chosen = sum(dot(pick, piece, 1, 1) for piece in split3(g_ref[...]))
    for t in range(2):
        out_ref[t * 4 * GROUP : (t + 1) * 4 * GROUP, :] = chosen


def lay_kernel(g_ref, out_ref):
    deep = g_ref.shape[1] // 8
    grow_row = lax.broadcasted_iota(jnp.int32, (GROUP, NG), 0)
    grow_col = lax.broadcasted_iota(jnp.int32, (GROUP, NG), 1)
    grow = (grow_row == grow_col // 8).astype(F32).astype(BF16)
    keep_row = lax.broadcasted_iota(jnp.int32, (deep * 8, NG), 0)
    keep_col = lax.broadcasted_iota(jnp.int32, (deep * 8, NG), 1)
    keep = keep_row % 8 == keep_col % 8
    for t in range(2):
        for p in range(4):
            rows = g_ref[pl.ds(t * 4 * GROUP + p, GROUP, stride=4), :].T
            wide = sum(dot(piece, grow) for piece in split3(rows))
            wide = jnp.where(keep, wide, 0.0)
            out_ref[t, p] = jnp.sum(wide.reshape(deep, 8, NG), axis=1)


def early_kernel(where_ref, alike_ref, table_ref, out_ref, all_ref):
    parity, slot = where_ref[0], where_ref[1]
    count, sides, _, deep, _ = alike_ref.shape
    all_ref[...] = jnp.zeros_like(all_ref)
    for k in range(count):
        for t in range(sides):
            at = ((2 * k + parity) * sides + t) * deep
            for p in range(4):
                all_ref[p, pl.ds(pl.multiple_of(at, 8), deep), :] = alike_ref[k, t, p]
    place, opposite_rows, opposite = table_ref[0], table_ref[1], table_ref[2]

    def placed(x):
        return sum(dot(place, piece) for piece in split2(x))

    def reflected(x):
        x = sum(dot(opposite_rows, piece) for piece in split2(x))
        return sum(dot(piece, opposite) for piece in split2(x))

    packed = slot == 0
    own, other = all_ref[0], all_ref[1]
    out_ref[0] = 0.5 * (placed(own) + reflected(jnp.where(packed, own, other)))
    out_ref[1] = 0.5 * (placed(jnp.where(packed, other, own)) + reflected(other))
    out_ref[2] = 0.5 * (placed(all_ref[2]) + reflected(all_ref[3]))


def late_gains(where_ref, halves, early_ref, table_ref, rows_ref, late_ref):
    parity, slot = where_ref[0], where_ref[1]
    half, sides, _, deep, _ = halves[0].shape
    size = sides * deep
    for k in range(2 * half):
        at = pl.multiple_of((2 * k + 1 - parity) * size, 16)
        for i in range(2):
            rows_ref[i, k * size : (k + 1) * size, :] = table_ref[i, pl.ds(at, size), :]
        for t in range(sides):
            for p in range(4):
                late_ref[p, k * size + t * deep : k * size + (t + 1) * deep, :] = halves[k // half][k % half, t, p]
    place, opposite_rows, opposite = rows_ref[0], rows_ref[1], table_ref[2]

    def placed(x):
        return sum(dot(place, piece, 0, 0) for piece in split2(x))

    def reflected(x):
        x = sum(dot(piece, opposite) for piece in split2(x))
        return sum(dot(opposite_rows, piece, 0, 0) for piece in split2(x))

    packed = slot == 0
    own, other = late_ref[0], late_ref[1]
    return (
        early_ref[0] + 0.5 * (placed(own) + reflected(jnp.where(packed, own, other))),
        early_ref[1] + 0.5 * (placed(jnp.where(packed, other, own)) + reflected(other)),
        early_ref[2] + 0.5 * (placed(late_ref[2]) + reflected(late_ref[3])),
    )


def call(kernel, out_shape, operands, name, flops=0, scratch=(), spaces=None, out_space=pltpu.VMEM, vmem=VMEM_LIMIT):
    moved = sum(x.size * x.dtype.itemsize for x in operands) + math.prod(out_shape) * 4
    spaces = spaces or [pltpu.VMEM] * len(operands)
    return pl.pallas_call(
        kernel,
        out_shape=jax.ShapeDtypeStruct(out_shape, F32),
        in_specs=[pl.BlockSpec(memory_space=space) for space in spaces],
        out_specs=pl.BlockSpec(memory_space=out_space),
        scratch_shapes=list(scratch),
        compiler_params=pltpu.CompilerParams(vmem_limit_bytes=vmem),
        cost_estimate=pl.CostEstimate(flops=flops, bytes_accessed=moved, transcendentals=0),
        name=name,
    )(*operands)


def spread(green):
    depth_count = lax.axis_size("z") * lax.axis_size("parity")
    deep = green.shape[0]
    pick = jnp.asarray(pick_table().astype(ml_dtypes.bfloat16))
    sent = call(
        pick_kernel,
        (2 * 4 * GROUP, deep * 8),
        (green.reshape(deep * 8, NZ), pick),
        "pick",
        flops=6 * 128**3,
        spaces=[pltpu.HBM] * 2,
        vmem=VMEM_ALL,
        scratch=[pltpu.VMEM((deep * 8, NZ), F32), pltpu.VMEM((4 * GROUP, NZ), BF16), pltpu.SemaphoreType.DMA((2,))],
    )
    sent = sent.reshape(2 * GROUP, 4, deep * 8)
    got = lax.all_to_all(sent, ("y_lo", "gy", "gz"), split_axis=0, concat_axis=0, tiled=True)
    pair = call(lay_kernel, (2, 4, deep, NG), (got.reshape(2 * 4 * GROUP, deep * 8),), "lay", flops=48 * 128 * 32 * 256)
    def along(value, by):
        return lax.ppermute(value, ("z", "parity"), [(i, (i + by) % depth_count) for i in range(depth_count)])

    alike = lax.all_gather(pair, "z")
    half = alike.shape[0] // 2
    return alike, along(alike[:half], 1), along(alike[half:], -1)


def on_device(charges, green):
    there, back = depth_tables()
    there = [jnp.asarray(t) for t in parts_of(there)]
    back = [jnp.asarray(t) for t in parts_of(back)]
    tables = [jnp.asarray(t) for table in plane_tables() for t in parts_of(table)]
    alike, *halves = spread(green)
    cells = ROWS * COLS
    chunks = HIGH // CHUNK
    sent = call(
        depth_kernel,
        (GROUP * ROWS, LANES),
        (charges.reshape(cells, NZ), *there),
        "depth",
        flops=6 * cells * NZ * NZ,
        spaces=[pltpu.HBM] * 3,
        vmem=VMEM_ALL,
        scratch=[pltpu.VMEM((cells, NZ), F32), pltpu.VMEM((2, 4 * GROUP, NZ), BF16), pltpu.SemaphoreType.DMA((2 + chunks,))],
    )
    sent = sent.reshape(GROUP, ROWS, LANES)
    got = lax.all_to_all(sent, ("gy", "gz"), split_axis=0, concat_axis=0, tiled=True)
    spectra = call(
        there_kernel,
        (2 * NG, 2 * NG),
        (got, *tables),
        "there",
        flops=6 * 16 * NG**3,
        scratch=[pltpu.VMEM((2 * NG, 2 * NG), F32)],
    )
    slot = lax.axis_index("gy") * GZ + lax.axis_index("gz")
    where = jnp.stack([lax.axis_index("parity"), slot]).astype(jnp.int32)
    place, opposite_rows, opposite = gain_tables()
    selections = jnp.asarray(np.stack([place, opposite_rows, opposite]).astype(ml_dtypes.bfloat16))
    turned = jnp.asarray(np.stack([place.T, opposite_rows.T, opposite]).astype(ml_dtypes.bfloat16))
    spectra, alike = lax.optimization_barrier((spectra, alike))
    early = call(
        early_kernel,
        (3, NG, NG),
        (where, alike, selections),
        "early",
        flops=36 * NG**3,
        scratch=[pltpu.VMEM((4, NG, NG), F32)],
        spaces=[pltpu.SMEM] + [pltpu.VMEM] * 2,
    )
    spectra, early, *halves = lax.optimization_barrier((spectra, early, *halves))
    late_rows = NG // 2
    sent = call(
        back_kernel,
        (GROUP, ROWS, LANES),
        (where, spectra, early, *halves, turned, *tables),
        "back",
        flops=6 * 20 * NG**3,
        spaces=[pltpu.SMEM] + [pltpu.VMEM] * 9,
        scratch=[pltpu.VMEM((2, late_rows, NG), BF16), pltpu.VMEM((4, late_rows, NG), F32)],
    )
    got = lax.all_to_all(sent, ("gy", "gz"), split_axis=0, concat_axis=0, tiled=True)
    out = call(
        cells_kernel,
        (cells, NZ),
        (got.reshape(GROUP * ROWS, LANES), *back),
        "cells",
        flops=6 * cells * NZ * NZ,
        scratch=[pltpu.VMEM((cells, NZ), F32), pltpu.SemaphoreType.DMA((chunks,))],
        out_space=pltpu.HBM,
    )
    return out.reshape(charges.shape)


def solution(mesh):
    rep = ("z", "parity", "y_lo")
    apart = jax.sharding.Mesh(mesh.devices.reshape(mesh.shape["rep"] // 4, 2, 2, GY, GZ), (*rep, "gy", "gz"))
    return jax.shard_map(
        on_device,
        mesh=apart,
        in_specs=(P((*rep, "gz"), "gy", None), P(rep, ("gy", "gz"), None)),
        out_specs=P((*rep, "gz"), "gy", None),
        check_vma=False,
    )
```

```python
import math

import jax
import jax.numpy as jnp
import ml_dtypes
import numpy as np
from jax import lax
from jax.experimental import pallas as pl
from jax.experimental.pallas import tpu as pltpu
from jax.sharding import PartitionSpec as P

NG = 256
NZ = 128
HALF = NZ // 2
GY = 8
GZ = 4
GROUP = GY * GZ
ROWS = NG // GZ
COLS = NG // GY
LANES = 128
LOW = LANES // COLS
HIGH = ROWS // LOW
CHUNK = 4

VMEM_LIMIT = 16 * 1024 * 1024
VMEM_ALL = 60 * 1024 * 1024
F32 = jnp.float32
BF16 = jnp.bfloat16


def parts_of(table, count=2):
    rest = np.asarray(table, np.float64)
    found = []
    for _ in range(count):
        piece = rest.astype(np.float32).astype(ml_dtypes.bfloat16)
        found.append(piece)
        rest = rest - piece.astype(np.float64)
    return found


def depth_tables():
    z = np.arange(NZ)
    there = np.zeros((2, 2, GROUP, NZ))
    back = np.zeros((2, 2, GROUP, NZ))
    for j in range(2):
        for s in range(GROUP):
            k = 2 * s + j
            angle = 2 * math.pi * ((k * z) % NZ) / NZ
            if k == 0:
                there[0, j, s] = 1.0
                there[1, j, s] = 1.0 - 2.0 * (z % 2)
                back[0, j, s] = 1.0
                back[1, j, s] = 2.0 * (z % 2) - 1.0
            else:
                there[0, j, s] = np.cos(angle)
                there[1, j, s] = -np.sin(angle)
                back[0, j, s] = 2 * np.cos(angle)
                back[1, j, s] = 2 * np.sin(angle)
    scale = 1.0 / (NG * NG * NZ)
    return there.reshape(4 * GROUP, NZ), back.reshape(4 * GROUP, NZ) * scale


def row_order():
    low, block, high = np.meshgrid(np.arange(LOW), np.arange(GZ), np.arange(HIGH), indexing="ij")
    return (block * ROWS + high * LOW + low).reshape(-1)


def plane_tables():
    index, order = np.arange(NG), row_order()
    angle = 2 * math.pi * (np.outer(index, index) % NG) / NG
    cos, sin = np.cos(angle), np.sin(angle)
    first = np.concatenate([cos[order][:, order], sin[order][:, order]], axis=1)
    return first, np.concatenate([cos, sin], axis=1)


def pick_table():
    pick = np.zeros((GROUP, 2, 2, NZ))
    for s in range(GROUP):
        for j in range(2):
            k = 2 * s + j
            pick[s, j, 0, k] = 1
            pick[s, j, 1, NZ // 2 if k == 0 else NZ - k] = 1
    return pick.reshape(4 * GROUP, NZ)


def gain_tables():
    index, order = np.arange(NG), row_order()
    place = (order[:, None] == index[None, :]).astype(np.float64)
    opposite = (index[:, None] == (-index[None, :]) % NG).astype(np.float64)
    return np.stack([place, place @ opposite, opposite])


def split2(x):
    high = x.astype(BF16)
    return high, (x - high.astype(F32)).astype(BF16)


def dot(a, b, da=1, db=0):
    return lax.dot_general(a, b, (((da,), (db,)), ((), ())), preferred_element_type=F32)


def dot3(a, b, da=1, db=0):
    return dot(a[0], b[0], da, db) + (dot(a[0], b[1], da, db) + dot(a[1], b[0], da, db))


def swap_blocks(arrays):
    lane = lax.broadcasted_iota(jnp.int32, arrays[0].shape, 1)
    low_half = lane < 2 * COLS
    even = (lane // COLS) % 2 == 0

    def turn(x, by):
        return pltpu.roll(x, by % LANES, 1)

    x0, x1, x2, x3 = arrays
    y0 = jnp.where(low_half, x0, turn(x2, 2 * COLS))
    y2 = jnp.where(low_half, turn(x0, 2 * COLS), x2)
    y1 = jnp.where(low_half, x1, turn(x3, 2 * COLS))
    y3 = jnp.where(low_half, turn(x1, 2 * COLS), x3)
    z0 = jnp.where(even, y0, turn(y1, COLS))
    z1 = jnp.where(even, turn(y0, -COLS), y1)
    z2 = jnp.where(even, y2, turn(y3, COLS))
    z3 = jnp.where(even, turn(y2, -COLS), y3)
    return z0, z1, z2, z3


def fetch(sources, targets, sems):
    copies = [pltpu.make_async_copy(a, b, sems.at[i]) for i, (a, b) in enumerate(zip(sources, targets, strict=True))]
    for copy in copies:
        copy.start()
    return copies


def wait(copies):
    for copy in copies:
        copy.wait()


def depth_kernel(q_hbm, high_hbm, low_hbm, out_ref, q_ref, w_ref, sems):
    size = CHUNK * LANES
    tables = fetch((high_hbm, low_hbm), (w_ref.at[0], w_ref.at[1]), sems)
    copies = [
        pltpu.make_async_copy(q_hbm.at[i * size : (i + 1) * size], q_ref.at[i * size : (i + 1) * size], sems.at[2 + i])
        for i in range(HIGH // CHUNK)
    ]
    for copy in copies:
        copy.start()
    wait(tables)
    w = (w_ref[0], w_ref[1])
    for h in range(HIGH):
        if h % CHUNK == 0:
            copies[h // CHUNK].wait()
        q = split2(q_ref[h * LANES : (h + 1) * LANES, :])
        t = dot3(w, q, 1, 1)
        for c in range(4):
            out_ref[pl.ds(c * HIGH + h, GROUP, stride=ROWS), :] = t[c * GROUP : (c + 1) * GROUP, :]


def cells_kernel(r_ref, high_ref, low_ref, out_hbm, out_ref, sems):
    w = (high_ref[...], low_ref[...])
    size = CHUNK * LANES
    copies = []
    for h in range(HIGH):
        t = jnp.concatenate([r_ref[pl.ds(c * HIGH + h, GROUP, stride=ROWS), :] for c in range(4)], axis=0)
        out_ref[h * LANES : (h + 1) * LANES, :] = dot3(split2(t.T), w)
        if h % CHUNK == CHUNK - 1:
            i = h // CHUNK
            copies.append(
                pltpu.make_async_copy(out_ref.at[i * size : (i + 1) * size], out_hbm.at[i * size : (i + 1) * size], sems.at[i])
            )
            copies[-1].start()
    wait(copies)


def stacked(high_ref, low_ref, sign):
    def stack(t):
        cos, sin = t[:, :NG], t[:, NG:]
        rows = [[cos, sin], [-sin, cos]] if sign > 0 else [[cos, -sin], [sin, cos]]
        return jnp.concatenate([jnp.concatenate(row, axis=1) for row in rows], axis=0)

    return stack(high_ref[...]), stack(low_ref[...])


def there_kernel(r_ref, lh, ll, rh, rl, out_ref, p_ref):
    for part in range(2):
        for j in range(2):
            c = 2 * part + j
            for gh in range(GY // LOW):
                arrays = [
                    r_ref[(gh * LOW + g) * GZ : (gh * LOW + g + 1) * GZ, c * HIGH : (c + 1) * HIGH, :].reshape(ROWS, LANES)
                    for g in range(LOW)
                ]
                for a, value in enumerate(swap_blocks(arrays)):
                    row, col = part * NG + a * ROWS, j * NG + gh * LANES
                    p_ref[row : row + ROWS, col : col + LANES] = value
    y = dot3(stacked(lh, ll, 1), split2(p_ref[...]))
    y = [jnp.concatenate([y[:NG, j * NG : (j + 1) * NG], y[NG:, j * NG : (j + 1) * NG]], axis=1) for j in range(2)]
    out_ref[...] = dot3(split2(jnp.concatenate(y, axis=0)), stacked(rh, rl, -1))


def across(t):
    return jnp.concatenate([t[0], t[0], t[1]], axis=1)


def down(t):
    return jnp.concatenate([t[0], t[1], t[0]], axis=0)


def back_kernel(where_ref, f_ref, early_ref, *refs):
    *parts, table_ref, lh, ll, rh, rl, out_ref, rows_ref, part_ref = refs
    columns = []
    for p, late in enumerate(share(parts, 1 - where_ref[0], where_ref[1], table_ref, rows_ref, part_ref)):
        gain = early_ref[p] + late
        rows = slice(p // 2 * NG, (p // 2 + 1) * NG)
        columns.append(jnp.concatenate([f_ref[rows, :NG] * gain, f_ref[rows, NG:] * -gain], axis=0))
    u = dot(across(stacked(lh, ll, 1)), down(split2(jnp.concatenate(columns, axis=1))))
    u = [split2(jnp.concatenate([u[:NG, p * NG : (p + 1) * NG], u[NG:, p * NG : (p + 1) * NG]], axis=1)) for p in range(3)]
    u = [across(t) for t in u]
    right = down(stacked(rh, rl, -1))
    v = {(0, 0): dot(u[0], right[:, :NG]), (1, 0): dot(u[1], right[:, NG:])}
    both = dot(u[2], right)
    v[0, 1], v[1, 1] = both[:, :NG], both[:, NG:]
    for (part, j), value in v.items():
        c = 2 * part + j
        for gh in range(GY // LOW):
            arrays = [value[a * ROWS : (a + 1) * ROWS, gh * LANES : (gh + 1) * LANES] for a in range(LOW)]
            for g, cells in enumerate(swap_blocks(arrays)):
                out_ref[(gh * LOW + g) * GZ : (gh * LOW + g + 1) * GZ, c * HIGH : (c + 1) * HIGH, :] = cells.reshape(GZ, HIGH, LANES)


def pick_kernel(g_hbm, pick_hbm, out_ref, g_ref, pick_ref, sems):
    wait(fetch((g_hbm, pick_hbm), (g_ref, pick_ref), sems))
    pick = pick_ref[...]
    chosen = sum(dot(pick, piece, 1, 1) for piece in split2(g_ref[...]))
    for t in range(2):
        out_ref[t * 4 * GROUP : (t + 1) * 4 * GROUP, :] = chosen


def lay_kernel(g_ref, out_ref):
    deep = g_ref.shape[1] // 8
    grow_row = lax.broadcasted_iota(jnp.int32, (GROUP, NG), 0)
    grow_col = lax.broadcasted_iota(jnp.int32, (GROUP, NG), 1)
    grow = (grow_row == grow_col // 8).astype(F32).astype(BF16)
    keep_row = lax.broadcasted_iota(jnp.int32, (deep * 8, NG), 0)
    keep_col = lax.broadcasted_iota(jnp.int32, (deep * 8, NG), 1)
    keep = keep_row % 8 == keep_col % 8
    for t in range(2):
        for p in range(4):
            rows = g_ref[pl.ds(t * 4 * GROUP + p, GROUP, stride=4), :].T
            wide = sum(dot(piece, grow) for piece in split2(rows))
            wide = jnp.where(keep, wide, 0.0)
            out_ref[t, p] = jnp.sum(wide.reshape(deep, 8, NG), axis=1)


def share(parts, other, slot, table_ref, rows_ref, part_ref):
    deep = parts[0].shape[2]
    blocks = [part.at[k] for part in parts for k in range(part.shape[0])]
    for k, block in enumerate(blocks):
        at = pl.multiple_of(((k // 2 * 2 + other) * 2 + k % 2) * deep, 16)
        rows = slice(k * deep, (k + 1) * deep)
        for i in range(2):
            rows_ref[i, rows, :] = table_ref[i, pl.ds(at, deep), :]
        for p in range(4):
            part_ref[p, rows, :] = block[p]
    place, opposite_rows, opposite = rows_ref[0], rows_ref[1], table_ref[2]

    def placed(x):
        return sum(dot(place, piece, 0, 0) for piece in split2(x))

    def reflected(x):
        x = sum(dot(piece, opposite) for piece in split2(x))
        return sum(dot(opposite_rows, piece, 0, 0) for piece in split2(x))

    packed = slot == 0
    own, far = part_ref[0], part_ref[1]
    return (
        0.5 * (placed(own) + reflected(jnp.where(packed, own, far))),
        0.5 * (placed(jnp.where(packed, far, own)) + reflected(far)),
        0.5 * (placed(part_ref[2]) + reflected(part_ref[3])),
    )


def early_kernel(where_ref, alike_ref, table_ref, out_ref, rows_ref, part_ref):
    for p, gain in enumerate(share((alike_ref,), where_ref[0], where_ref[1], table_ref, rows_ref, part_ref)):
        out_ref[p] = gain


def call(kernel, out_shape, operands, name, flops=0, scratch=(), spaces=None, out_space=pltpu.VMEM, vmem=VMEM_LIMIT):
    moved = sum(x.size * x.dtype.itemsize for x in operands) + math.prod(out_shape) * 4
    spaces = spaces or [pltpu.VMEM] * len(operands)
    return pl.pallas_call(
        kernel,
        out_shape=jax.ShapeDtypeStruct(out_shape, F32),
        in_specs=[pl.BlockSpec(memory_space=space) for space in spaces],
        out_specs=pl.BlockSpec(memory_space=out_space),
        scratch_shapes=list(scratch),
        compiler_params=pltpu.CompilerParams(vmem_limit_bytes=vmem),
        cost_estimate=pl.CostEstimate(flops=flops, bytes_accessed=moved, transcendentals=0),
        name=name,
    )(*operands)


def spread(green):
    depth_count = lax.axis_size("z") * lax.axis_size("parity")
    deep = green.shape[0]
    pick = jnp.asarray(pick_table().astype(ml_dtypes.bfloat16))
    sent = call(
        pick_kernel,
        (2 * 4 * GROUP, deep * 8),
        (green.reshape(deep * 8, NZ), pick),
        "pick",
        flops=6 * 128**3,
        spaces=[pltpu.HBM] * 2,
        vmem=VMEM_ALL,
        scratch=[pltpu.VMEM((deep * 8, NZ), F32), pltpu.VMEM((4 * GROUP, NZ), BF16), pltpu.SemaphoreType.DMA((2,))],
    )
    sent = sent.reshape(2 * GROUP, 4, deep * 8)
    got = lax.all_to_all(sent, ("y_lo", "gy", "gz"), split_axis=0, concat_axis=0, tiled=True)
    pair = call(lay_kernel, (2, 4, deep, NG), (got.reshape(2 * 4 * GROUP, deep * 8),), "lay", flops=48 * 128 * 32 * 256)
    def along(value, by):
        return lax.ppermute(value, ("z", "parity"), [(i, (i + by) % depth_count) for i in range(depth_count)])

    alike = lax.all_gather(pair, "z")
    alike = alike.reshape(-1, *alike.shape[2:])
    first = alike.shape[0] // 2 + 1
    return alike, along(alike[:first], 1), along(alike[first:], -1)


def on_device(charges, green):
    there, back = depth_tables()
    there = [jnp.asarray(t) for t in parts_of(there)]
    back = [jnp.asarray(t) for t in parts_of(back)]
    tables = [jnp.asarray(t) for table in plane_tables() for t in parts_of(table)]
    alike, *parts = spread(green)
    cells = ROWS * COLS
    chunks = HIGH // CHUNK
    sent = call(
        depth_kernel,
        (GROUP * ROWS, LANES),
        (charges.reshape(cells, NZ), *there),
        "depth",
        flops=6 * cells * NZ * NZ,
        spaces=[pltpu.HBM] * 3,
        vmem=VMEM_ALL,
        scratch=[pltpu.VMEM((cells, NZ), F32), pltpu.VMEM((2, 4 * GROUP, NZ), BF16), pltpu.SemaphoreType.DMA((2 + chunks,))],
    )
    sent = sent.reshape(GROUP, ROWS, LANES)
    got = lax.all_to_all(sent, ("gy", "gz"), split_axis=0, concat_axis=0, tiled=True)
    spectra = call(
        there_kernel,
        (2 * NG, 2 * NG),
        (got, *tables),
        "there",
        flops=6 * 16 * NG**3,
        scratch=[pltpu.VMEM((2 * NG, 2 * NG), F32)],
    )
    slot = lax.axis_index("gy") * GZ + lax.axis_index("gz")
    where = jnp.stack([lax.axis_index("parity"), slot]).astype(jnp.int32)
    place, opposite_rows, opposite = gain_tables()
    turned = jnp.asarray(np.stack([place.T, opposite_rows.T, opposite]).astype(ml_dtypes.bfloat16))
    spectra, alike = lax.optimization_barrier((spectra, alike))
    share_scratch = [pltpu.VMEM((2, NG // 2, NG), BF16), pltpu.VMEM((4, NG // 2, NG), F32)]
    early = call(
        early_kernel,
        (3, NG, NG),
        (where, alike, turned),
        "early",
        flops=18 * NG**3,
        scratch=share_scratch,
        spaces=[pltpu.SMEM] + [pltpu.VMEM] * 2,
    )
    spectra, early, *parts = lax.optimization_barrier((spectra, early, *parts))
    sent = call(
        back_kernel,
        (GROUP, ROWS, LANES),
        (where, spectra, early, *parts, turned, *tables),
        "back",
        flops=6 * 20 * NG**3,
        spaces=[pltpu.SMEM] + [pltpu.VMEM] * 9,
        scratch=share_scratch,
    )
    got = lax.all_to_all(sent, ("gy", "gz"), split_axis=0, concat_axis=0, tiled=True)
    out = call(
        cells_kernel,
        (cells, NZ),
        (got.reshape(GROUP * ROWS, LANES), *back),
        "cells",
        flops=6 * cells * NZ * NZ,
        scratch=[pltpu.VMEM((cells, NZ), F32), pltpu.SemaphoreType.DMA((chunks,))],
        out_space=pltpu.HBM,
    )
    return out.reshape(charges.shape)


def solution(mesh):
    rep = ("z", "parity", "y_lo")
    apart = jax.sharding.Mesh(mesh.devices.reshape(mesh.shape["rep"] // 4, 2, 2, GY, GZ), (*rep, "gy", "gz"))
    return jax.shard_map(
        on_device,
        mesh=apart,
        in_specs=(P((*rep, "gz"), "gy", None), P(rep, ("gy", "gz"), None)),
        out_specs=P((*rep, "gz"), "gy", None),
        check_vma=False,
    )
```

```python
import math

import jax
import jax.numpy as jnp
import ml_dtypes
import numpy as np
from jax import lax
from jax.experimental import pallas as pl
from jax.experimental.pallas import tpu as pltpu
from jax.sharding import PartitionSpec as P

NG = 256
NZ = 128
HALF = NZ // 2
GY = 8
GZ = 4
GROUP = GY * GZ
ROWS = NG // GZ
COLS = NG // GY
LANES = 128
LOW = LANES // COLS
HIGH = ROWS // LOW
CHUNK = 4
OUT_CHUNK = 2

VMEM_LIMIT = 16 * 1024 * 1024
VMEM_ALL = 60 * 1024 * 1024
F32 = jnp.float32
BF16 = jnp.bfloat16


def parts_of(table, count=2):
    rest = np.asarray(table, np.float64)
    found = []
    for _ in range(count):
        piece = rest.astype(np.float32).astype(ml_dtypes.bfloat16)
        found.append(piece)
        rest = rest - piece.astype(np.float64)
    return found


def depth_tables():
    z = np.arange(NZ)
    there = np.zeros((2, 2, GROUP, NZ))
    back = np.zeros((2, 2, GROUP, NZ))
    for j in range(2):
        for s in range(GROUP):
            k = 2 * s + j
            angle = 2 * math.pi * ((k * z) % NZ) / NZ
            if k == 0:
                there[0, j, s] = 1.0
                there[1, j, s] = 1.0 - 2.0 * (z % 2)
                back[0, j, s] = 1.0
                back[1, j, s] = 2.0 * (z % 2) - 1.0
            else:
                there[0, j, s] = np.cos(angle)
                there[1, j, s] = -np.sin(angle)
                back[0, j, s] = 2 * np.cos(angle)
                back[1, j, s] = 2 * np.sin(angle)
    scale = 1.0 / (NG * NG * NZ)
    return there.reshape(4 * GROUP, NZ), back.reshape(4 * GROUP, NZ) * scale


def row_order():
    low, block, high = np.meshgrid(np.arange(LOW), np.arange(GZ), np.arange(HIGH), indexing="ij")
    return (block * ROWS + high * LOW + low).reshape(-1)


def plane_tables():
    index, order = np.arange(NG), row_order()
    angle = 2 * math.pi * (np.outer(index, index) % NG) / NG
    cos, sin = np.cos(angle), np.sin(angle)
    first = np.concatenate([cos[order][:, order], sin[order][:, order]], axis=1)
    return first, np.concatenate([cos, sin], axis=1)


def pick_table():
    pick = np.zeros((GROUP, 2, 2, NZ))
    for s in range(GROUP):
        for j in range(2):
            k = 2 * s + j
            pick[s, j, 0, k] = 1
            pick[s, j, 1, NZ // 2 if k == 0 else NZ - k] = 1
    return pick.reshape(4 * GROUP, NZ)


def gain_tables():
    index, order = np.arange(NG), row_order()
    place = (order[:, None] == index[None, :]).astype(np.float64)
    opposite = (index[:, None] == (-index[None, :]) % NG).astype(np.float64)
    return np.stack([place, place @ opposite, opposite])


def split2(x):
    high = x.astype(BF16)
    return high, (x - high.astype(F32)).astype(BF16)


def dot(a, b, da=1, db=0):
    return lax.dot_general(a, b, (((da,), (db,)), ((), ())), preferred_element_type=F32)


def dot3(a, b, da=1, db=0):
    return dot(a[0], b[0], da, db) + (dot(a[0], b[1], da, db) + dot(a[1], b[0], da, db))


def swap_blocks(arrays):
    lane = lax.broadcasted_iota(jnp.int32, arrays[0].shape, 1)
    low_half = lane < 2 * COLS
    even = (lane // COLS) % 2 == 0

    def turn(x, by):
        return pltpu.roll(x, by % LANES, 1)

    x0, x1, x2, x3 = arrays
    y0 = jnp.where(low_half, x0, turn(x2, 2 * COLS))
    y2 = jnp.where(low_half, turn(x0, 2 * COLS), x2)
    y1 = jnp.where(low_half, x1, turn(x3, 2 * COLS))
    y3 = jnp.where(low_half, turn(x1, 2 * COLS), x3)
    z0 = jnp.where(even, y0, turn(y1, COLS))
    z1 = jnp.where(even, turn(y0, -COLS), y1)
    z2 = jnp.where(even, y2, turn(y3, COLS))
    z3 = jnp.where(even, turn(y2, -COLS), y3)
    return z0, z1, z2, z3


def fetch(sources, targets, sems):
    copies = [pltpu.make_async_copy(a, b, sems.at[i]) for i, (a, b) in enumerate(zip(sources, targets, strict=True))]
    for copy in copies:
        copy.start()
    return copies


def wait(copies):
    for copy in copies:
        copy.wait()


def depth_kernel(q_hbm, high_hbm, low_hbm, out_ref, q_ref, w_ref, sems):
    size = CHUNK * LANES
    tables = fetch((high_hbm, low_hbm), (w_ref.at[0], w_ref.at[1]), sems)
    copies = [
        pltpu.make_async_copy(q_hbm.at[i * size : (i + 1) * size], q_ref.at[i * size : (i + 1) * size], sems.at[2 + i])
        for i in range(HIGH // CHUNK)
    ]
    for copy in copies:
        copy.start()
    wait(tables)
    w = (w_ref[0], w_ref[1])
    for h in range(HIGH):
        if h % CHUNK == 0:
            copies[h // CHUNK].wait()
        q = split2(q_ref[h * LANES : (h + 1) * LANES, :])
        t = dot3(w, q, 1, 1)
        for c in range(4):
            out_ref[pl.ds(c * HIGH + h, GROUP, stride=ROWS), :] = t[c * GROUP : (c + 1) * GROUP, :]


def cells_kernel(r_ref, high_ref, low_ref, out_hbm, out_ref, sems):
    w = (high_ref[...], low_ref[...])
    size = OUT_CHUNK * LANES
    copies = []
    for h in range(HIGH):
        t = jnp.concatenate([r_ref[pl.ds(c * HIGH + h, GROUP, stride=ROWS), :] for c in range(4)], axis=0)
        out_ref[h * LANES : (h + 1) * LANES, :] = dot3(split2(t), w, 0, 0)
        if h % OUT_CHUNK == OUT_CHUNK - 1:
            i = h // OUT_CHUNK
            copies.append(
                pltpu.make_async_copy(out_ref.at[i * size : (i + 1) * size], out_hbm.at[i * size : (i + 1) * size], sems.at[i])
            )
            copies[-1].start()
    wait(copies)


def stacked(high_ref, low_ref, sign):
    def stack(t):
        cos, sin = t[:, :NG], t[:, NG:]
        rows = [[cos, sin], [-sin, cos]] if sign > 0 else [[cos, -sin], [sin, cos]]
        return jnp.concatenate([jnp.concatenate(row, axis=1) for row in rows], axis=0)

    return stack(high_ref[...]), stack(low_ref[...])


def there_kernel(r_ref, lh, ll, rh, rl, out_ref, p_ref):
    for part in range(2):
        for j in range(2):
            c = 2 * part + j
            for gh in range(GY // LOW):
                arrays = [
                    r_ref[(gh * LOW + g) * GZ : (gh * LOW + g + 1) * GZ, c * HIGH : (c + 1) * HIGH, :].reshape(ROWS, LANES)
                    for g in range(LOW)
                ]
                for a, value in enumerate(swap_blocks(arrays)):
                    row, col = part * NG + a * ROWS, j * NG + gh * LANES
                    p_ref[row : row + ROWS, col : col + LANES] = value
    y = dot3(stacked(lh, ll, 1), split2(p_ref[...]))
    y = [jnp.concatenate([y[:NG, j * NG : (j + 1) * NG], y[NG:, j * NG : (j + 1) * NG]], axis=1) for j in range(2)]
    out_ref[...] = dot3(split2(jnp.concatenate(y, axis=0)), stacked(rh, rl, -1))


def across(t):
    return jnp.concatenate([t[0], t[0], t[1]], axis=1)


def down(t):
    return jnp.concatenate([t[0], t[1], t[0]], axis=0)


def back_kernel(where_ref, f_ref, early_ref, *refs):
    *parts, table_ref, lh, ll, rh, rl, out_ref, rows_ref, part_ref = refs
    columns = []
    for p, late in enumerate(share(parts, 1 - where_ref[0], where_ref[1], table_ref, rows_ref, part_ref)):
        gain = early_ref[p] + late
        rows = slice(p // 2 * NG, (p // 2 + 1) * NG)
        columns.append(jnp.concatenate([f_ref[rows, :NG] * gain, f_ref[rows, NG:] * -gain], axis=0))
    u = dot(across(stacked(lh, ll, 1)), down(split2(jnp.concatenate(columns, axis=1))))
    u = [split2(jnp.concatenate([u[:NG, p * NG : (p + 1) * NG], u[NG:, p * NG : (p + 1) * NG]], axis=1)) for p in range(3)]
    u = [across(t) for t in u]
    right = down(stacked(rh, rl, -1))
    v = {(0, 0): dot(u[0], right[:, :NG]), (1, 0): dot(u[1], right[:, NG:])}
    both = dot(u[2], right)
    v[0, 1], v[1, 1] = both[:, :NG], both[:, NG:]
    for (part, j), value in v.items():
        c = 2 * part + j
        for gh in range(GY // LOW):
            arrays = [value[a * ROWS : (a + 1) * ROWS, gh * LANES : (gh + 1) * LANES] for a in range(LOW)]
            for g, cells in enumerate(swap_blocks(arrays)):
                out_ref[(gh * LOW + g) * GZ : (gh * LOW + g + 1) * GZ, c * HIGH : (c + 1) * HIGH, :] = cells.reshape(GZ, HIGH, LANES)


def pick_kernel(g_hbm, pick_hbm, out_ref, g_ref, pick_ref, sems):
    wait(fetch((g_hbm, pick_hbm), (g_ref, pick_ref), sems))
    pick = pick_ref[...]
    chosen = sum(dot(pick, piece, 1, 1) for piece in split2(g_ref[...]))
    for t in range(2):
        out_ref[t * 4 * GROUP : (t + 1) * 4 * GROUP, :] = chosen


def lay_kernel(g_ref, out_ref):
    deep = g_ref.shape[1] // 8
    grow_row = lax.broadcasted_iota(jnp.int32, (GROUP, NG), 0)
    grow_col = lax.broadcasted_iota(jnp.int32, (GROUP, NG), 1)
    grow = (grow_row == grow_col // 8).astype(F32).astype(BF16)
    keep_row = lax.broadcasted_iota(jnp.int32, (deep * 8, NG), 0)
    keep_col = lax.broadcasted_iota(jnp.int32, (deep * 8, NG), 1)
    keep = keep_row % 8 == keep_col % 8
    for t in range(2):
        for p in range(4):
            rows = g_ref[pl.ds(t * 4 * GROUP + p, GROUP, stride=4), :].T
            wide = sum(dot(piece, grow) for piece in split2(rows))
            wide = jnp.where(keep, wide, 0.0)
            out_ref[t, p] = jnp.sum(wide.reshape(deep, 8, NG), axis=1)


def share(parts, other, slot, table_ref, rows_ref, part_ref):
    deep = parts[0].shape[2]
    blocks = [part.at[k] for part in parts for k in range(part.shape[0])]
    for k, block in enumerate(blocks):
        at = pl.multiple_of(((k // 2 * 2 + other) * 2 + k % 2) * deep, 16)
        rows = slice(k * deep, (k + 1) * deep)
        for i in range(2):
            rows_ref[i, rows, :] = table_ref[i, pl.ds(at, deep), :]
        for p in range(4):
            part_ref[p, rows, :] = block[p]
    place, opposite_rows, opposite = rows_ref[0], rows_ref[1], table_ref[2]

    def placed(x):
        return sum(dot(place, piece, 0, 0) for piece in split2(x))

    def reflected(x):
        x = sum(dot(piece, opposite) for piece in split2(x))
        return sum(dot(opposite_rows, piece, 0, 0) for piece in split2(x))

    packed = slot == 0
    own, far = part_ref[0], part_ref[1]
    return (
        0.5 * (placed(own) + reflected(jnp.where(packed, own, far))),
        0.5 * (placed(jnp.where(packed, far, own)) + reflected(far)),
        0.5 * (placed(part_ref[2]) + reflected(part_ref[3])),
    )


def early_kernel(where_ref, alike_ref, table_ref, out_ref, rows_ref, part_ref):
    for p, gain in enumerate(share((alike_ref,), where_ref[0], where_ref[1], table_ref, rows_ref, part_ref)):
        out_ref[p] = gain


def call(kernel, out_shape, operands, name, flops=0, scratch=(), spaces=None, out_space=pltpu.VMEM, vmem=VMEM_LIMIT):
    moved = sum(x.size * x.dtype.itemsize for x in operands) + math.prod(out_shape) * 4
    spaces = spaces or [pltpu.VMEM] * len(operands)
    return pl.pallas_call(
        kernel,
        out_shape=jax.ShapeDtypeStruct(out_shape, F32),
        in_specs=[pl.BlockSpec(memory_space=space) for space in spaces],
        out_specs=pl.BlockSpec(memory_space=out_space),
        scratch_shapes=list(scratch),
        compiler_params=pltpu.CompilerParams(vmem_limit_bytes=vmem),
        cost_estimate=pl.CostEstimate(flops=flops, bytes_accessed=moved, transcendentals=0),
        name=name,
    )(*operands)


def spread(green):
    depth_count = lax.axis_size("z") * lax.axis_size("parity")
    deep = green.shape[0]
    pick = jnp.asarray(pick_table().astype(ml_dtypes.bfloat16))
    sent = call(
        pick_kernel,
        (2 * 4 * GROUP, deep * 8),
        (green.reshape(deep * 8, NZ), pick),
        "pick",
        flops=6 * 128**3,
        spaces=[pltpu.HBM] * 2,
        vmem=VMEM_ALL,
        scratch=[pltpu.VMEM((deep * 8, NZ), F32), pltpu.VMEM((4 * GROUP, NZ), BF16), pltpu.SemaphoreType.DMA((2,))],
    )
    sent = sent.reshape(2 * GROUP, 4, deep * 8)
    got = lax.all_to_all(sent, ("y_lo", "gy", "gz"), split_axis=0, concat_axis=0, tiled=True)
    pair = call(lay_kernel, (2, 4, deep, NG), (got.reshape(2 * 4 * GROUP, deep * 8),), "lay", flops=48 * 128 * 32 * 256)
    def along(value, by):
        return lax.ppermute(value, ("z", "parity"), [(i, (i + by) % depth_count) for i in range(depth_count)])

    alike = lax.all_gather(pair, "z")
    alike = alike.reshape(-1, *alike.shape[2:])
    first = alike.shape[0] // 2 + 1
    return alike, along(alike[:first], 1), along(alike[first:], -1)


def on_device(charges, green):
    there, back = depth_tables()
    there = [jnp.asarray(t) for t in parts_of(there)]
    back = [jnp.asarray(t) for t in parts_of(back)]
    tables = [jnp.asarray(t) for table in plane_tables() for t in parts_of(table)]
    alike, *parts = spread(green)
    cells = ROWS * COLS
    chunks = HIGH // CHUNK
    sent = call(
        depth_kernel,
        (GROUP * ROWS, LANES),
        (charges.reshape(cells, NZ), *there),
        "depth",
        flops=6 * cells * NZ * NZ,
        spaces=[pltpu.HBM] * 3,
        vmem=VMEM_ALL,
        scratch=[pltpu.VMEM((cells, NZ), F32), pltpu.VMEM((2, 4 * GROUP, NZ), BF16), pltpu.SemaphoreType.DMA((2 + chunks,))],
    )
    sent = sent.reshape(GROUP, ROWS, LANES)
    got = lax.all_to_all(sent, ("gy", "gz"), split_axis=0, concat_axis=0, tiled=True)
    spectra = call(
        there_kernel,
        (2 * NG, 2 * NG),
        (got, *tables),
        "there",
        flops=6 * 16 * NG**3,
        scratch=[pltpu.VMEM((2 * NG, 2 * NG), F32)],
    )
    slot = lax.axis_index("gy") * GZ + lax.axis_index("gz")
    where = jnp.stack([lax.axis_index("parity"), slot]).astype(jnp.int32)
    place, opposite_rows, opposite = gain_tables()
    turned = jnp.asarray(np.stack([place.T, opposite_rows.T, opposite]).astype(ml_dtypes.bfloat16))
    spectra, alike = lax.optimization_barrier((spectra, alike))
    share_scratch = [pltpu.VMEM((2, NG // 2, NG), BF16), pltpu.VMEM((4, NG // 2, NG), F32)]
    early = call(
        early_kernel,
        (3, NG, NG),
        (where, alike, turned),
        "early",
        flops=18 * NG**3,
        scratch=share_scratch,
        spaces=[pltpu.SMEM] + [pltpu.VMEM] * 2,
    )
    spectra, early, *parts = lax.optimization_barrier((spectra, early, *parts))
    sent = call(
        back_kernel,
        (GROUP, ROWS, LANES),
        (where, spectra, early, *parts, turned, *tables),
        "back",
        flops=6 * 20 * NG**3,
        spaces=[pltpu.SMEM] + [pltpu.VMEM] * 9,
        scratch=share_scratch,
    )
    got = lax.all_to_all(sent, ("gy", "gz"), split_axis=0, concat_axis=0, tiled=True)
    out = call(
        cells_kernel,
        (cells, NZ),
        (got.reshape(GROUP * ROWS, LANES), *back),
        "cells",
        flops=6 * cells * NZ * NZ,
        scratch=[pltpu.VMEM((cells, NZ), F32), pltpu.SemaphoreType.DMA((HIGH // OUT_CHUNK,))],
        out_space=pltpu.HBM,
    )
    return out.reshape(charges.shape)


def solution(mesh):
    rep = ("z", "parity", "y_lo")
    apart = jax.sharding.Mesh(mesh.devices.reshape(mesh.shape["rep"] // 4, 2, 2, GY, GZ), (*rep, "gy", "gz"))
    return jax.shard_map(
        on_device,
        mesh=apart,
        in_specs=(P((*rep, "gz"), "gy", None), P(rep, ("gy", "gz"), None)),
        out_specs=P((*rep, "gz"), "gy", None),
        check_vma=False,
    )
```

```python
import math

import jax
import jax.numpy as jnp
import ml_dtypes
import numpy as np
from jax import lax
from jax.experimental import pallas as pl
from jax.experimental.pallas import tpu as pltpu
from jax.sharding import PartitionSpec as P

NG = 256
NZ = 128
HALF = NZ // 2
GY = 8
GZ = 4
GROUP = GY * GZ
ROWS = NG // GZ
COLS = NG // GY
LANES = 128
LOW = LANES // COLS
HIGH = ROWS // LOW
CHUNK = 4

VMEM_LIMIT = 16 * 1024 * 1024
VMEM_ALL = 60 * 1024 * 1024
F32 = jnp.float32
BF16 = jnp.bfloat16


def parts_of(table, count=2):
    rest = np.asarray(table, np.float64)
    found = []
    for _ in range(count):
        piece = rest.astype(np.float32).astype(ml_dtypes.bfloat16)
        found.append(piece)
        rest = rest - piece.astype(np.float64)
    return found


def depth_tables():
    z = np.arange(NZ)
    there = np.zeros((2, 2, GROUP, NZ))
    back = np.zeros((2, 2, GROUP, NZ))
    for j in range(2):
        for s in range(GROUP):
            k = 2 * s + j
            angle = 2 * math.pi * ((k * z) % NZ) / NZ
            if k == 0:
                there[0, j, s] = 1.0
                there[1, j, s] = 1.0 - 2.0 * (z % 2)
                back[0, j, s] = 1.0
                back[1, j, s] = 2.0 * (z % 2) - 1.0
            else:
                there[0, j, s] = np.cos(angle)
                there[1, j, s] = -np.sin(angle)
                back[0, j, s] = 2 * np.cos(angle)
                back[1, j, s] = 2 * np.sin(angle)
    scale = 1.0 / (NG * NG * NZ)
    return there.reshape(4 * GROUP, NZ), back.reshape(4 * GROUP, NZ) * scale


def row_order():
    low, block, high = np.meshgrid(np.arange(LOW), np.arange(GZ), np.arange(HIGH), indexing="ij")
    return (block * ROWS + high * LOW + low).reshape(-1)


def plane_tables():
    index, order = np.arange(NG), row_order()
    angle = 2 * math.pi * (np.outer(index, index) % NG) / NG
    cos, sin = np.cos(angle), np.sin(angle)
    first = np.concatenate([cos[order][:, order], sin[order][:, order]], axis=1)
    return first, np.concatenate([cos, sin], axis=1)


def pick_table():
    pick = np.zeros((GROUP, 2, 2, NZ))
    for s in range(GROUP):
        for j in range(2):
            k = 2 * s + j
            pick[s, j, 0, k] = 1
            pick[s, j, 1, NZ // 2 if k == 0 else NZ - k] = 1
    return pick.reshape(4 * GROUP, NZ)


def gain_tables():
    index, order = np.arange(NG), row_order()
    place = (order[:, None] == index[None, :]).astype(np.float64)
    opposite = (index[:, None] == (-index[None, :]) % NG).astype(np.float64)
    return np.stack([place, place @ opposite, opposite])


def split2(x):
    high = x.astype(BF16)
    return high, (x - high.astype(F32)).astype(BF16)


def split3(x):
    high = x.astype(BF16)
    rest = x - high.astype(F32)
    mid = rest.astype(BF16)
    return high, mid, (rest - mid.astype(F32)).astype(BF16)


def dot(a, b, da=1, db=0):
    return lax.dot_general(a, b, (((da,), (db,)), ((), ())), preferred_element_type=F32)


def dot3(a, b, da=1, db=0):
    return dot(a[0], b[0], da, db) + (dot(a[0], b[1], da, db) + dot(a[1], b[0], da, db))


def swap_blocks(arrays):
    lane = lax.broadcasted_iota(jnp.int32, arrays[0].shape, 1)
    low_half = lane < 2 * COLS
    even = (lane // COLS) % 2 == 0

    def turn(x, by):
        return pltpu.roll(x, by % LANES, 1)

    x0, x1, x2, x3 = arrays
    y0 = jnp.where(low_half, x0, turn(x2, 2 * COLS))
    y2 = jnp.where(low_half, turn(x0, 2 * COLS), x2)
    y1 = jnp.where(low_half, x1, turn(x3, 2 * COLS))
    y3 = jnp.where(low_half, turn(x1, 2 * COLS), x3)
    z0 = jnp.where(even, y0, turn(y1, COLS))
    z1 = jnp.where(even, turn(y0, -COLS), y1)
    z2 = jnp.where(even, y2, turn(y3, COLS))
    z3 = jnp.where(even, turn(y2, -COLS), y3)
    return z0, z1, z2, z3


def fetch(sources, targets, sems):
    copies = [pltpu.make_async_copy(a, b, sems.at[i]) for i, (a, b) in enumerate(zip(sources, targets, strict=True))]
    for copy in copies:
        copy.start()
    return copies


def wait(copies):
    for copy in copies:
        copy.wait()


def depth_kernel(q_hbm, high_hbm, low_hbm, out_ref, q_ref, w_ref, sems):
    size = CHUNK * LANES
    tables = fetch((high_hbm, low_hbm), (w_ref.at[0], w_ref.at[1]), sems)
    copies = [
        pltpu.make_async_copy(q_hbm.at[i * size : (i + 1) * size], q_ref.at[i * size : (i + 1) * size], sems.at[2 + i])
        for i in range(HIGH // CHUNK)
    ]
    for copy in copies:
        copy.start()
    wait(tables)
    w = (w_ref[0], w_ref[1])
    for h in range(HIGH):
        if h % CHUNK == 0:
            copies[h // CHUNK].wait()
        q = split2(q_ref[h * LANES : (h + 1) * LANES, :])
        t = dot3(w, q, 1, 1)
        for c in range(4):
            out_ref[pl.ds(c * HIGH + h, GROUP, stride=ROWS), :] = t[c * GROUP : (c + 1) * GROUP, :]


def cells_kernel(r_ref, high_ref, low_ref, out_hbm, out_ref, sems):
    w = (high_ref[...], low_ref[...])
    size = CHUNK * LANES
    copies = []
    for h in range(HIGH):
        t = jnp.concatenate([r_ref[pl.ds(c * HIGH + h, GROUP, stride=ROWS), :] for c in range(4)], axis=0)
        out_ref[h * LANES : (h + 1) * LANES, :] = dot3(split2(t.T), w)
        if h % CHUNK == CHUNK - 1:
            i = h // CHUNK
            copies.append(
                pltpu.make_async_copy(out_ref.at[i * size : (i + 1) * size], out_hbm.at[i * size : (i + 1) * size], sems.at[i])
            )
            copies[-1].start()
    wait(copies)


def stacked(high_ref, low_ref, sign):
    def stack(t):
        cos, sin = t[:, :NG], t[:, NG:]
        rows = [[cos, sin], [-sin, cos]] if sign > 0 else [[cos, -sin], [sin, cos]]
        return jnp.concatenate([jnp.concatenate(row, axis=1) for row in rows], axis=0)

    return stack(high_ref[...]), stack(low_ref[...])


def there_kernel(r_ref, lh, ll, rh, rl, out_ref, p_ref):
    for part in range(2):
        for j in range(2):
            c = 2 * part + j
            for gh in range(GY // LOW):
                arrays = [
                    r_ref[(gh * LOW + g) * GZ : (gh * LOW + g + 1) * GZ, c * HIGH : (c + 1) * HIGH, :].reshape(ROWS, LANES)
                    for g in range(LOW)
                ]
                for a, value in enumerate(swap_blocks(arrays)):
                    row, col = part * NG + a * ROWS, j * NG + gh * LANES
                    p_ref[row : row + ROWS, col : col + LANES] = value
    y = dot3(stacked(lh, ll, 1), split2(p_ref[...]))
    y = [jnp.concatenate([y[:NG, j * NG : (j + 1) * NG], y[NG:, j * NG : (j + 1) * NG]], axis=1) for j in range(2)]
    out_ref[...] = dot3(split2(jnp.concatenate(y, axis=0)), stacked(rh, rl, -1))


def back_kernel(f_ref, gain_ref, lh, ll, rh, rl, out_ref):
    columns = []
    for p in range(3):
        rows = slice(p // 2 * NG, (p // 2 + 1) * NG)
        gain = gain_ref[p]
        columns.append(jnp.concatenate([f_ref[rows, :NG] * gain, f_ref[rows, NG:] * -gain], axis=0))
    u = dot3(stacked(lh, ll, 1), split2(jnp.concatenate(columns, axis=1)))
    u = [split2(jnp.concatenate([u[:NG, p * NG : (p + 1) * NG], u[NG:, p * NG : (p + 1) * NG]], axis=1)) for p in range(3)]
    right = stacked(rh, rl, -1)
    v = {(0, 0): dot3(u[0], tuple(t[:, :NG] for t in right)), (1, 0): dot3(u[1], tuple(t[:, NG:] for t in right))}
    both = dot3(u[2], right)
    v[0, 1], v[1, 1] = both[:, :NG], both[:, NG:]
    for (part, j), value in v.items():
        c = 2 * part + j
        for gh in range(GY // LOW):
            arrays = [value[a * ROWS : (a + 1) * ROWS, gh * LANES : (gh + 1) * LANES] for a in range(LOW)]
            for g, cells in enumerate(swap_blocks(arrays)):
                out_ref[(gh * LOW + g) * GZ : (gh * LOW + g + 1) * GZ, c * HIGH : (c + 1) * HIGH, :] = cells.reshape(GZ, HIGH, LANES)


def pick_kernel(g_hbm, pick_hbm, out_ref, g_ref, pick_ref, sems):
    wait(fetch((g_hbm, pick_hbm), (g_ref, pick_ref), sems))
    pick = pick_ref[...]
    chosen = sum(dot(pick, piece, 1, 1) for piece in split3(g_ref[...]))
    for t in range(2):
        out_ref[t * 4 * GROUP : (t + 1) * 4 * GROUP, :] = chosen


def lay_kernel(g_ref, out_ref):
    deep = g_ref.shape[1] // 8
    grow_row = lax.broadcasted_iota(jnp.int32, (GROUP, NG), 0)
    grow_col = lax.broadcasted_iota(jnp.int32, (GROUP, NG), 1)
    grow = (grow_row == grow_col // 8).astype(F32).astype(BF16)
    keep_row = lax.broadcasted_iota(jnp.int32, (deep * 8, NG), 0)
    keep_col = lax.broadcasted_iota(jnp.int32, (deep * 8, NG), 1)
    keep = keep_row % 8 == keep_col % 8
    for t in range(2):
        for p in range(4):
            rows = g_ref[pl.ds(t * 4 * GROUP + p, GROUP, stride=4), :].T
            wide = sum(dot(piece, grow) for piece in split3(rows))
            wide = jnp.where(keep, wide, 0.0)
            out_ref[t, p] = jnp.sum(wide.reshape(deep, 8, NG), axis=1)


def gain_kernel(where_ref, *refs):
    pair, low, high, far, below, above, table_ref, out_ref, all_ref = refs
    pieces = [pair, below.at[0], low, below.at[1], far, above.at[1], high, above.at[0]]
    depth, slot = where_ref[0], where_ref[1]
    count = len(pieces)
    deep = NG // (2 * count)
    for step, piece in enumerate(pieces):
        shift = step if step <= count // 2 else step - count
        owner = lax.rem(depth - shift + count, count)
        for t in range(2):
            at = (owner * 2 + t) * deep
            for p in range(4):
                all_ref[p, pl.ds(pl.multiple_of(at, 8), deep), :] = piece[t, p]
    place, opposite_rows, opposite = table_ref[0], table_ref[1], table_ref[2]

    def placed(x):
        return sum(dot(place, piece) for piece in split2(x))

    def reflected(x):
        x = sum(dot(opposite_rows, piece) for piece in split2(x))
        return sum(dot(piece, opposite) for piece in split2(x))

    packed = slot == 0
    own, other = all_ref[0], all_ref[1]
    out_ref[0] = 0.5 * (placed(own) + reflected(jnp.where(packed, own, other)))
    out_ref[1] = 0.5 * (placed(jnp.where(packed, other, own)) + reflected(other))
    out_ref[2] = 0.5 * (placed(all_ref[2]) + reflected(all_ref[3]))


def call(kernel, out_shape, operands, name, flops=0, scratch=(), spaces=None, out_space=pltpu.VMEM, vmem=VMEM_LIMIT):
    moved = sum(x.size * x.dtype.itemsize for x in operands) + math.prod(out_shape) * 4
    spaces = spaces or [pltpu.VMEM] * len(operands)
    return pl.pallas_call(
        kernel,
        out_shape=jax.ShapeDtypeStruct(out_shape, F32),
        in_specs=[pl.BlockSpec(memory_space=space) for space in spaces],
        out_specs=pl.BlockSpec(memory_space=out_space),
        scratch_shapes=list(scratch),
        compiler_params=pltpu.CompilerParams(vmem_limit_bytes=vmem),
        cost_estimate=pl.CostEstimate(flops=flops, bytes_accessed=moved, transcendentals=0),
        name=name,
    )(*operands)


def spread(green):
    depth_count = lax.axis_size("z")
    deep = green.shape[0]
    pick = jnp.asarray(pick_table().astype(ml_dtypes.bfloat16))
    sent = call(
        pick_kernel,
        (2 * 4 * GROUP, deep * 8),
        (green.reshape(deep * 8, NZ), pick),
        "pick",
        flops=6 * 128**3,
        spaces=[pltpu.HBM] * 2,
        vmem=VMEM_ALL,
        scratch=[pltpu.VMEM((deep * 8, NZ), F32), pltpu.VMEM((4 * GROUP, NZ), BF16), pltpu.SemaphoreType.DMA((2,))],
    )
    sent = sent.reshape(2 * GROUP, 4, deep * 8)
    got = lax.all_to_all(sent, ("y_lo", "gy", "gz"), split_axis=0, concat_axis=0, tiled=True)
    pair = call(lay_kernel, (2, 4, deep, NG), (got.reshape(2 * 4 * GROUP, deep * 8),), "lay", flops=48 * 128 * 32 * 256)
    def along(value, by):
        return lax.ppermute(value, "z", [(i, (i + by) % depth_count) for i in range(depth_count)])

    low, high = along(pair, 2), along(pair, -2)
    opposite = along(low, 2)
    below, above = along(jnp.stack([pair, low]), 1), along(jnp.stack([pair, high]), -1)
    pieces = [pair, low, high, opposite, below, above]
    return pieces


def gains(pieces):
    slot = lax.axis_index("gy") * GZ + lax.axis_index("gz")
    where = jnp.stack([lax.axis_index("z"), slot]).astype(jnp.int32)
    selections = jnp.asarray(gain_tables().astype(ml_dtypes.bfloat16))
    return call(
        gain_kernel,
        (3, NG, NG),
        (where, *pieces, selections),
        "gain",
        flops=54 * NG**3,
        scratch=[pltpu.VMEM((4, NG, NG), F32)],
        spaces=[pltpu.SMEM] + [pltpu.VMEM] * 7,
    )


def on_device(charges, green):
    there, back = depth_tables()
    there = [jnp.asarray(t) for t in parts_of(there)]
    back = [jnp.asarray(t) for t in parts_of(back)]
    tables = [jnp.asarray(t) for table in plane_tables() for t in parts_of(table)]
    pieces = spread(green)
    cells = ROWS * COLS
    chunks = HIGH // CHUNK
    sent = call(
        depth_kernel,
        (GROUP * ROWS, LANES),
        (charges.reshape(cells, NZ), *there),
        "depth",
        flops=6 * cells * NZ * NZ,
        spaces=[pltpu.HBM] * 3,
        vmem=VMEM_ALL,
        scratch=[pltpu.VMEM((cells, NZ), F32), pltpu.VMEM((2, 4 * GROUP, NZ), BF16), pltpu.SemaphoreType.DMA((2 + chunks,))],
    )
    sent = sent.reshape(GROUP, ROWS, LANES)
    got = lax.all_to_all(sent, ("gy", "gz"), split_axis=0, concat_axis=0, tiled=True)
    spectra = call(
        there_kernel,
        (2 * NG, 2 * NG),
        (got, *tables),
        "there",
        flops=6 * 16 * NG**3,
        scratch=[pltpu.VMEM((2 * NG, 2 * NG), F32)],
    )
    spectra, *pieces[3:] = lax.optimization_barrier((spectra, *pieces[3:]))
    sent = call(
        back_kernel,
        (GROUP, ROWS, LANES),
        (spectra, gains(pieces), *tables),
        "back",
        flops=6 * 20 * NG**3,
    )
    got = lax.all_to_all(sent, ("gy", "gz"), split_axis=0, concat_axis=0, tiled=True)
    out = call(
        cells_kernel,
        (cells, NZ),
        (got.reshape(GROUP * ROWS, LANES), *back),
        "cells",
        flops=6 * cells * NZ * NZ,
        scratch=[pltpu.VMEM((cells, NZ), F32), pltpu.SemaphoreType.DMA((chunks,))],
        out_space=pltpu.HBM,
    )
    return out.reshape(charges.shape)


def solution(mesh):
    apart = jax.sharding.Mesh(
        mesh.devices.reshape(mesh.shape["rep"] // 2, 2, mesh.shape["gy"], mesh.shape["gz"]), ("z", "y_lo", "gy", "gz")
    )
    return jax.shard_map(
        on_device,
        mesh=apart,
        in_specs=(P(("z", "y_lo", "gz"), "gy", None), P(("z", "y_lo"), ("gy", "gz"), None)),
        out_specs=P(("z", "y_lo", "gz"), "gy", None),
        check_vma=False,
    )
```

```python
import math

import jax
import jax.numpy as jnp
import ml_dtypes
import numpy as np
from jax import lax
from jax.experimental import pallas as pl
from jax.experimental.pallas import tpu as pltpu
from jax.sharding import PartitionSpec as P

NG = 256
NZ = 128
HALF = NZ // 2
GY = 8
GZ = 4
GROUP = GY * GZ
ROWS = NG // GZ
COLS = NG // GY
LANES = 128
LOW = LANES // COLS
HIGH = ROWS // LOW
CHUNK = 4

VMEM_LIMIT = 16 * 1024 * 1024
VMEM_ALL = 60 * 1024 * 1024
F32 = jnp.float32
BF16 = jnp.bfloat16


def parts_of(table, count=2):
    rest = np.asarray(table, np.float64)
    found = []
    for _ in range(count):
        piece = rest.astype(np.float32).astype(ml_dtypes.bfloat16)
        found.append(piece)
        rest = rest - piece.astype(np.float64)
    return found


def depth_tables():
    z = np.arange(NZ)
    there = np.zeros((2, 2, GROUP, NZ))
    back = np.zeros((2, 2, GROUP, NZ))
    for j in range(2):
        for s in range(GROUP):
            k = 2 * s + j
            angle = 2 * math.pi * ((k * z) % NZ) / NZ
            if k == 0:
                there[0, j, s] = 1.0
                there[1, j, s] = 1.0 - 2.0 * (z % 2)
                back[0, j, s] = 1.0
                back[1, j, s] = 2.0 * (z % 2) - 1.0
            else:
                there[0, j, s] = np.cos(angle)
                there[1, j, s] = -np.sin(angle)
                back[0, j, s] = 2 * np.cos(angle)
                back[1, j, s] = 2 * np.sin(angle)
    scale = 1.0 / (NG * NG * NZ)
    return there.reshape(4 * GROUP, NZ), back.reshape(4 * GROUP, NZ) * scale


def row_order():
    low, block, high = np.meshgrid(np.arange(LOW), np.arange(GZ), np.arange(HIGH), indexing="ij")
    return (block * ROWS + high * LOW + low).reshape(-1)


def plane_tables():
    index, order = np.arange(NG), row_order()
    angle = 2 * math.pi * (np.outer(index, index) % NG) / NG
    cos, sin = np.cos(angle), np.sin(angle)
    first = np.concatenate([cos[order][:, order], sin[order][:, order]], axis=1)
    return first, np.concatenate([cos, sin], axis=1)


def pick_table():
    pick = np.zeros((GROUP, 2, 2, NZ))
    for s in range(GROUP):
        for j in range(2):
            k = 2 * s + j
            pick[s, j, 0, k] = 1
            pick[s, j, 1, NZ // 2 if k == 0 else NZ - k] = 1
    return pick.reshape(4 * GROUP, NZ)


def gain_tables():
    index, order = np.arange(NG), row_order()
    place = (order[:, None] == index[None, :]).astype(np.float64)
    opposite = (index[:, None] == (-index[None, :]) % NG).astype(np.float64)
    return np.stack([place, place @ opposite, opposite])


def split2(x):
    high = x.astype(BF16)
    return high, (x - high.astype(F32)).astype(BF16)


def split3(x):
    high = x.astype(BF16)
    rest = x - high.astype(F32)
    mid = rest.astype(BF16)
    return high, mid, (rest - mid.astype(F32)).astype(BF16)


def dot(a, b, da=1, db=0):
    return lax.dot_general(a, b, (((da,), (db,)), ((), ())), preferred_element_type=F32)


def dot3(a, b, da=1, db=0):
    return dot(a[0], b[0], da, db) + (dot(a[0], b[1], da, db) + dot(a[1], b[0], da, db))


def swap_blocks(arrays):
    lane = lax.broadcasted_iota(jnp.int32, arrays[0].shape, 1)
    low_half = lane < 2 * COLS
    even = (lane // COLS) % 2 == 0

    def turn(x, by):
        return pltpu.roll(x, by % LANES, 1)

    x0, x1, x2, x3 = arrays
    y0 = jnp.where(low_half, x0, turn(x2, 2 * COLS))
    y2 = jnp.where(low_half, turn(x0, 2 * COLS), x2)
    y1 = jnp.where(low_half, x1, turn(x3, 2 * COLS))
    y3 = jnp.where(low_half, turn(x1, 2 * COLS), x3)
    z0 = jnp.where(even, y0, turn(y1, COLS))
    z1 = jnp.where(even, turn(y0, -COLS), y1)
    z2 = jnp.where(even, y2, turn(y3, COLS))
    z3 = jnp.where(even, turn(y2, -COLS), y3)
    return z0, z1, z2, z3


def fetch(sources, targets, sems):
    copies = [pltpu.make_async_copy(a, b, sems.at[i]) for i, (a, b) in enumerate(zip(sources, targets, strict=True))]
    for copy in copies:
        copy.start()
    return copies


def wait(copies):
    for copy in copies:
        copy.wait()


def depth_kernel(q_hbm, high_hbm, low_hbm, out_ref, q_ref, w_ref, sems):
    size = CHUNK * LANES
    tables = fetch((high_hbm, low_hbm), (w_ref.at[0], w_ref.at[1]), sems)
    copies = [
        pltpu.make_async_copy(q_hbm.at[i * size : (i + 1) * size], q_ref.at[i * size : (i + 1) * size], sems.at[2 + i])
        for i in range(HIGH // CHUNK)
    ]
    for copy in copies:
        copy.start()
    wait(tables)
    w = (w_ref[0], w_ref[1])
    for h in range(HIGH):
        if h % CHUNK == 0:
            copies[h // CHUNK].wait()
        q = split2(q_ref[h * LANES : (h + 1) * LANES, :])
        t = dot3(w, q, 1, 1)
        for c in range(4):
            out_ref[pl.ds(c * HIGH + h, GROUP, stride=ROWS), :] = t[c * GROUP : (c + 1) * GROUP, :]


def cells_kernel(r_ref, high_ref, low_ref, out_hbm, out_ref, sems):
    w = (high_ref[...], low_ref[...])
    size = CHUNK * LANES
    copies = []
    for h in range(HIGH):
        t = jnp.concatenate([r_ref[pl.ds(c * HIGH + h, GROUP, stride=ROWS), :] for c in range(4)], axis=0)
        out_ref[h * LANES : (h + 1) * LANES, :] = dot3(split2(t.T), w)
        if h % CHUNK == CHUNK - 1:
            i = h // CHUNK
            copies.append(
                pltpu.make_async_copy(out_ref.at[i * size : (i + 1) * size], out_hbm.at[i * size : (i + 1) * size], sems.at[i])
            )
            copies[-1].start()
    wait(copies)


def stacked(high_ref, low_ref, sign):
    def stack(t):
        cos, sin = t[:, :NG], t[:, NG:]
        rows = [[cos, sin], [-sin, cos]] if sign > 0 else [[cos, -sin], [sin, cos]]
        return jnp.concatenate([jnp.concatenate(row, axis=1) for row in rows], axis=0)

    return stack(high_ref[...]), stack(low_ref[...])


def there_kernel(r_ref, lh, ll, rh, rl, out_ref, p_ref):
    for part in range(2):
        for j in range(2):
            c = 2 * part + j
            for gh in range(GY // LOW):
                arrays = [
                    r_ref[(gh * LOW + g) * GZ : (gh * LOW + g + 1) * GZ, c * HIGH : (c + 1) * HIGH, :].reshape(ROWS, LANES)
                    for g in range(LOW)
                ]
                for a, value in enumerate(swap_blocks(arrays)):
                    row, col = part * NG + a * ROWS, j * NG + gh * LANES
                    p_ref[row : row + ROWS, col : col + LANES] = value
    y = dot3(stacked(lh, ll, 1), split2(p_ref[...]))
    y = [jnp.concatenate([y[:NG, j * NG : (j + 1) * NG], y[NG:, j * NG : (j + 1) * NG]], axis=1) for j in range(2)]
    out_ref[...] = dot3(split2(jnp.concatenate(y, axis=0)), stacked(rh, rl, -1))


def across(t):
    return jnp.concatenate([t[0], t[0], t[1]], axis=1)


def down(t):
    return jnp.concatenate([t[0], t[1], t[0]], axis=0)


def back_kernel(where_ref, f_ref, early_ref, *refs):
    *parts, table_ref, lh, ll, rh, rl, out_ref, rows_ref, late_ref = refs
    columns = []
    for p, gain in enumerate(late_gains(where_ref, parts, early_ref, table_ref, rows_ref, late_ref)):
        rows = slice(p // 2 * NG, (p // 2 + 1) * NG)
        columns.append(jnp.concatenate([f_ref[rows, :NG] * gain, f_ref[rows, NG:] * -gain], axis=0))
    u = dot(across(stacked(lh, ll, 1)), down(split2(jnp.concatenate(columns, axis=1))))
    u = [split2(jnp.concatenate([u[:NG, p * NG : (p + 1) * NG], u[NG:, p * NG : (p + 1) * NG]], axis=1)) for p in range(3)]
    u = [across(t) for t in u]
    right = down(stacked(rh, rl, -1))
    v = {(0, 0): dot(u[0], right[:, :NG]), (1, 0): dot(u[1], right[:, NG:])}
    both = dot(u[2], right)
    v[0, 1], v[1, 1] = both[:, :NG], both[:, NG:]
    for (part, j), value in v.items():
        c = 2 * part + j
        for gh in range(GY // LOW):
            arrays = [value[a * ROWS : (a + 1) * ROWS, gh * LANES : (gh + 1) * LANES] for a in range(LOW)]
            for g, cells in enumerate(swap_blocks(arrays)):
                out_ref[(gh * LOW + g) * GZ : (gh * LOW + g + 1) * GZ, c * HIGH : (c + 1) * HIGH, :] = cells.reshape(GZ, HIGH, LANES)


def pick_kernel(g_hbm, pick_hbm, out_ref, g_ref, pick_ref, sems):
    wait(fetch((g_hbm, pick_hbm), (g_ref, pick_ref), sems))
    pick = pick_ref[...]
    chosen = sum(dot(pick, piece, 1, 1) for piece in split3(g_ref[...]))
    for t in range(2):
        out_ref[t * 4 * GROUP : (t + 1) * 4 * GROUP, :] = chosen


def lay_kernel(g_ref, out_ref):
    deep = g_ref.shape[1] // 8
    grow_row = lax.broadcasted_iota(jnp.int32, (GROUP, NG), 0)
    grow_col = lax.broadcasted_iota(jnp.int32, (GROUP, NG), 1)
    grow = (grow_row == grow_col // 8).astype(F32).astype(BF16)
    keep_row = lax.broadcasted_iota(jnp.int32, (deep * 8, NG), 0)
    keep_col = lax.broadcasted_iota(jnp.int32, (deep * 8, NG), 1)
    keep = keep_row % 8 == keep_col % 8
    for t in range(2):
        for p in range(4):
            rows = g_ref[pl.ds(t * 4 * GROUP + p, GROUP, stride=4), :].T
            wide = sum(dot(piece, grow) for piece in split3(rows))
            wide = jnp.where(keep, wide, 0.0)
            out_ref[t, p] = jnp.sum(wide.reshape(deep, 8, NG), axis=1)


def early_kernel(where_ref, alike_ref, table_ref, out_ref, all_ref):
    parity, slot = where_ref[0], where_ref[1]
    count, _, deep, _ = alike_ref.shape
    all_ref[...] = jnp.zeros_like(all_ref)
    for k in range(count):
        at = ((k // 2 * 2 + parity) * 2 + k % 2) * deep
        for p in range(4):
            all_ref[p, pl.ds(pl.multiple_of(at, 8), deep), :] = alike_ref[k, p]
    place, opposite_rows, opposite = table_ref[0], table_ref[1], table_ref[2]

    def placed(x):
        return sum(dot(place, piece) for piece in split2(x))

    def reflected(x):
        x = sum(dot(opposite_rows, piece) for piece in split2(x))
        return sum(dot(piece, opposite) for piece in split2(x))

    packed = slot == 0
    own, other = all_ref[0], all_ref[1]
    out_ref[0] = 0.5 * (placed(own) + reflected(jnp.where(packed, own, other)))
    out_ref[1] = 0.5 * (placed(jnp.where(packed, other, own)) + reflected(other))
    out_ref[2] = 0.5 * (placed(all_ref[2]) + reflected(all_ref[3]))


def late_gains(where_ref, parts, early_ref, table_ref, rows_ref, late_ref):
    parity, slot = where_ref[0], where_ref[1]
    first, _, deep, _ = parts[0].shape
    for k in range(first + parts[1].shape[0]):
        at = pl.multiple_of(((k // 2 * 2 + 1 - parity) * 2 + k % 2) * deep, 16)
        rows = slice(k * deep, (k + 1) * deep)
        for i in range(2):
            rows_ref[i, rows, :] = table_ref[i, pl.ds(at, deep), :]
        part, n = (parts[0], k) if k < first else (parts[1], k - first)
        for p in range(4):
            late_ref[p, rows, :] = part[n, p]
    place, opposite_rows, opposite = rows_ref[0], rows_ref[1], table_ref[2]

    def placed(x):
        return sum(dot(place, piece, 0, 0) for piece in split2(x))

    def reflected(x):
        x = sum(dot(piece, opposite) for piece in split2(x))
        return sum(dot(opposite_rows, piece, 0, 0) for piece in split2(x))

    packed = slot == 0
    own, other = late_ref[0], late_ref[1]
    return (
        early_ref[0] + 0.5 * (placed(own) + reflected(jnp.where(packed, own, other))),
        early_ref[1] + 0.5 * (placed(jnp.where(packed, other, own)) + reflected(other)),
        early_ref[2] + 0.5 * (placed(late_ref[2]) + reflected(late_ref[3])),
    )


def call(kernel, out_shape, operands, name, flops=0, scratch=(), spaces=None, out_space=pltpu.VMEM, vmem=VMEM_LIMIT):
    moved = sum(x.size * x.dtype.itemsize for x in operands) + math.prod(out_shape) * 4
    spaces = spaces or [pltpu.VMEM] * len(operands)
    return pl.pallas_call(
        kernel,
        out_shape=jax.ShapeDtypeStruct(out_shape, F32),
        in_specs=[pl.BlockSpec(memory_space=space) for space in spaces],
        out_specs=pl.BlockSpec(memory_space=out_space),
        scratch_shapes=list(scratch),
        compiler_params=pltpu.CompilerParams(vmem_limit_bytes=vmem),
        cost_estimate=pl.CostEstimate(flops=flops, bytes_accessed=moved, transcendentals=0),
        name=name,
    )(*operands)


def spread(green):
    depth_count = lax.axis_size("z") * lax.axis_size("parity")
    deep = green.shape[0]
    pick = jnp.asarray(pick_table().astype(ml_dtypes.bfloat16))
    sent = call(
        pick_kernel,
        (2 * 4 * GROUP, deep * 8),
        (green.reshape(deep * 8, NZ), pick),
        "pick",
        flops=6 * 128**3,
        spaces=[pltpu.HBM] * 2,
        vmem=VMEM_ALL,
        scratch=[pltpu.VMEM((deep * 8, NZ), F32), pltpu.VMEM((4 * GROUP, NZ), BF16), pltpu.SemaphoreType.DMA((2,))],
    )
    sent = sent.reshape(2 * GROUP, 4, deep * 8)
    got = lax.all_to_all(sent, ("y_lo", "gy", "gz"), split_axis=0, concat_axis=0, tiled=True)
    pair = call(lay_kernel, (2, 4, deep, NG), (got.reshape(2 * 4 * GROUP, deep * 8),), "lay", flops=48 * 128 * 32 * 256)
    def along(value, by):
        return lax.ppermute(value, ("z", "parity"), [(i, (i + by) % depth_count) for i in range(depth_count)])

    alike = lax.all_gather(pair, "z")
    alike = alike.reshape(-1, *alike.shape[2:])
    first = alike.shape[0] // 2 + 1
    return alike, along(alike[:first], 1), along(alike[first:], -1)


def on_device(charges, green):
    there, back = depth_tables()
    there = [jnp.asarray(t) for t in parts_of(there)]
    back = [jnp.asarray(t) for t in parts_of(back)]
    tables = [jnp.asarray(t) for table in plane_tables() for t in parts_of(table)]
    alike, *parts = spread(green)
    cells = ROWS * COLS
    chunks = HIGH // CHUNK
    sent = call(
        depth_kernel,
        (GROUP * ROWS, LANES),
        (charges.reshape(cells, NZ), *there),
        "depth",
        flops=6 * cells * NZ * NZ,
        spaces=[pltpu.HBM] * 3,
        vmem=VMEM_ALL,
        scratch=[pltpu.VMEM((cells, NZ), F32), pltpu.VMEM((2, 4 * GROUP, NZ), BF16), pltpu.SemaphoreType.DMA((2 + chunks,))],
    )
    sent = sent.reshape(GROUP, ROWS, LANES)
    got = lax.all_to_all(sent, ("gy", "gz"), split_axis=0, concat_axis=0, tiled=True)
    spectra = call(
        there_kernel,
        (2 * NG, 2 * NG),
        (got, *tables),
        "there",
        flops=6 * 16 * NG**3,
        scratch=[pltpu.VMEM((2 * NG, 2 * NG), F32)],
    )
    slot = lax.axis_index("gy") * GZ + lax.axis_index("gz")
    where = jnp.stack([lax.axis_index("parity"), slot]).astype(jnp.int32)
    place, opposite_rows, opposite = gain_tables()
    selections = jnp.asarray(np.stack([place, opposite_rows, opposite]).astype(ml_dtypes.bfloat16))
    turned = jnp.asarray(np.stack([place.T, opposite_rows.T, opposite]).astype(ml_dtypes.bfloat16))
    spectra, alike = lax.optimization_barrier((spectra, alike))
    early = call(
        early_kernel,
        (3, NG, NG),
        (where, alike, selections),
        "early",
        flops=36 * NG**3,
        scratch=[pltpu.VMEM((4, NG, NG), F32)],
        spaces=[pltpu.SMEM] + [pltpu.VMEM] * 2,
    )
    spectra, early, *parts = lax.optimization_barrier((spectra, early, *parts))
    late_rows = NG // 2
    sent = call(
        back_kernel,
        (GROUP, ROWS, LANES),
        (where, spectra, early, *parts, turned, *tables),
        "back",
        flops=6 * 20 * NG**3,
        spaces=[pltpu.SMEM] + [pltpu.VMEM] * 9,
        scratch=[pltpu.VMEM((2, late_rows, NG), BF16), pltpu.VMEM((4, late_rows, NG), F32)],
    )
    got = lax.all_to_all(sent, ("gy", "gz"), split_axis=0, concat_axis=0, tiled=True)
    out = call(
        cells_kernel,
        (cells, NZ),
        (got.reshape(GROUP * ROWS, LANES), *back),
        "cells",
        flops=6 * cells * NZ * NZ,
        scratch=[pltpu.VMEM((cells, NZ), F32), pltpu.SemaphoreType.DMA((chunks,))],
        out_space=pltpu.HBM,
    )
    return out.reshape(charges.shape)


def solution(mesh):
    rep = ("z", "parity", "y_lo")
    apart = jax.sharding.Mesh(mesh.devices.reshape(mesh.shape["rep"] // 4, 2, 2, GY, GZ), (*rep, "gy", "gz"))
    return jax.shard_map(
        on_device,
        mesh=apart,
        in_specs=(P((*rep, "gz"), "gy", None), P(rep, ("gy", "gz"), None)),
        out_specs=P((*rep, "gz"), "gy", None),
        check_vma=False,
    )
```
